32 devices in a mesh: dp: 8 (over z, y), mp: 4 (over x, core).
Axes of the slice: x: 2, y: 2, z: 4, core: 2. Of those that a mesh axis runs over, the one named last changes fastest.
Arguments:
- hidden_in: bfloat16 [3072, 2048], P(('dp', 'mp')), may hold values from -12 to 12
- segment_ids: int32 [8, 384], P('dp'), may hold values from 0 to 7, never falling along the last dimension, each value on 1 to 192 neighbouring positions
- page_table: int32 [8, 3], P('dp'), may hold values from 0 to 2, each once within a row
- qkv_master: float32 [2048, 6144], P(('dp', 'mp')), may hold values from -0.3 to 0.3
- up_master: float32 [2048, 8192], P(('dp', 'mp')), may hold values from -0.125 to 0.125
- dense_weight: bfloat16 [2048, 2048], P('mp'), may hold values from -0.125 to 0.125
Outputs:
- hidden_out: bfloat16 [3072, 2048], P(('dp', 'mp'))
- activated: bfloat16 [3072, 8192], P('dp', 'mp')
- cache_pages: bfloat16 [24, 2, 16, 128, 128], P('dp', None, 'mp')
The draws below stay inside these ranges and needn't reach their ends.
Inputs may be any that keep to these rules, and one draw needn't show every extreme that they name: `segment_ids`: within a group segment ids never fall; each request holds 1 to 192 tokens and one holds exactly that many. `page_table`: each row names every slot of its group once.
All inputs are finite; a program needn't handle non-finite values.
Results may differ from the reference program's by a relative error of at most 0.015.
Values may be sent and summed in bfloat16 or wider, within the bound.
No kernel may reach another device: no remote copies, remote signals or barrier semaphores. Data moves between devices by JAX's collectives and lax.ppermute only.
A program may use at most 64 MiB of HBM per device.

```python
import math
import jax
import jax.numpy as jnp
import numpy as np
from jax import lax

D = 2048
H = 16
HD = 128
FF = 8192
PAGE = 128
PAGES_GRP = 3
SEGS = 8
TOK_GRP = 384
TOKENS = 3072
PAGES = 24
N_DP = 8
N_MP = 4


def shared_signs(key):
    row_signs = jax.random.rademacher(jax.random.fold_in(key, 11), (D,), dtype=jnp.int32).astype(jnp.float32)
    head_signs = jax.random.rademacher(jax.random.fold_in(key, 12), (H, HD), dtype=jnp.int32).astype(jnp.float32)
    return (row_signs, head_signs)


def draw_hidden_in(key, part):
    cluster_len = 6
    groups = TOKENS // TOK_GRP
    noise = jax.random.normal(jax.random.fold_in(key, 31), (groups, TOK_GRP, D), jnp.float32)
    starts = jax.random.randint(jax.random.fold_in(key, 32), (groups, 1), 0, TOK_GRP - cluster_len + 1)
    strength = jax.random.uniform(jax.random.fold_in(key, 33), (groups, 1, 1), jnp.float32, 1.0, 2.0)
    places = jnp.arange(TOK_GRP)[None, :]
    inside = ((places >= starts) & (places < starts + cluster_len)).astype(jnp.float32)[:, :, None]
    row_signs, head_signs = shared_signs(key)
    values = noise + inside * strength * row_signs[None, None, :]
    values = jnp.clip(values, -12.0, 12.0)
    return values.reshape(TOKENS, D).astype(jnp.bfloat16)


def draw_qkv_master(key, part):
    scale = 1.0 / math.sqrt(D)
    base = jax.random.normal(jax.random.fold_in(key, 41), (D, H, 3, HD), jnp.float32) * scale
    row_signs, head_signs = shared_signs(key)
    amplitude = math.sqrt(450.0 * math.sqrt(HD) / D) / (math.sqrt(D) * math.sqrt(HD))
    extra = amplitude * row_signs[:, None, None] * head_signs[None, :, :]
    zeros = jnp.zeros_like(extra)
    added = jnp.stack([extra, extra, zeros], 2)
    values = jnp.clip(base + added, -0.3, 0.3)
    return values.reshape(D, 3 * D)


def steps_of(own_key, shape, cuts, smallest, high):
    loudness, own = 1.0, jax.random.fold_in(own_key, 6)
    for position, shards_of in cuts:
        draws = jnp.exp(jax.random.uniform(jax.random.fold_in(own, position), (shards_of,), jnp.float32, smallest / len(cuts), high / len(cuts)))
        loudness = loudness * jnp.repeat(draws, shape[position] // shards_of).reshape([-1 if axis == position else 1 for axis in range(len(shape))])
    return loudness


def length_profile(count, total, limit, lean):
    portions = [(1 << 20) // math.isqrt(standing ** lean) + 1 for standing in range(2, count + 1)]
    spare, holding = total - limit - (count - 1), [1] * (count - 1)
    while spare > 0:
        movable = [i for i in range(count - 1) if holding[i] < limit]
        mass, budget = sum([portions[i] for i in movable]), spare
        for i in movable:
            more = min(limit - holding[i], max(1, budget * portions[i] // mass), spare)
            holding[i] = holding[i] + more
            spare = spare - more
    return np.array([limit] + holding)


def uneven_parts(key, number_of, total, bound, skew):
    if number_of == 2:
        one = jax.random.randint(key, (), max(1, total - bound), min(bound, total - 1) + 1)
        return jnp.stack([one, total - one])
    tallies = jnp.asarray(length_profile(number_of, total, bound, skew), jnp.int32)
    pairs = (number_of - 1) // 2
    donor, taker = tallies[1:1 + 2 * pairs:2], tallies[2:2 + 2 * pairs:2]
    slack = jnp.minimum(donor - 1, bound - taker)
    moved = jax.random.randint(jax.random.fold_in(key, 1), (pairs,), 0, 1 << 20) % (slack + 1)
    tallies = tallies.at[1:1 + 2 * pairs:2].set(donor - moved).at[2:2 + 2 * pairs:2].set(taker + moved)
    return tallies[jax.random.permutation(jax.random.fold_in(key, 2), number_of)]


def centred(own_key, extent, deviation, most, cuts=(), kind=jnp.bfloat16):
    loudness = steps_of(own_key, extent, cuts, -0.22, 0.18) if cuts else 1.0
    values = jax.random.normal(own_key, extent, jnp.float32) * deviation * loudness
    return jnp.minimum(jnp.maximum(values, -most), most).astype(kind)


def setup_inputs(seed: int = 0) -> dict:
    seeds = jax.random.split(jax.random.key(seed), 7)
    return {
        "hidden_in": draw_hidden_in(jax.random.fold_in(seeds[6], 71), 0),
        "segment_ids": jax.vmap(lambda own: jnp.searchsorted(jnp.cumsum(uneven_parts(own, SEGS, TOK_GRP, TOK_GRP // 2, 2)), jnp.arange(TOK_GRP), side="right"))(jax.random.split(seeds[1], N_DP)).reshape((N_DP, TOK_GRP)).astype(jnp.int32),
        "page_table": jax.vmap(lambda own: jax.random.permutation(own, PAGES_GRP))(jax.random.split(seeds[2], N_DP)).reshape((N_DP, PAGES_GRP)).astype(jnp.int32),
        "qkv_master": draw_qkv_master(jax.random.fold_in(seeds[6], 71), 0),
        "up_master": centred(seeds[4], (D, FF), D ** -0.5, 0.125, ((0, 32),), jnp.float32),
        "dense_weight": centred(seeds[5], (D, D), D ** -0.5, 0.125, ((0, 4),)),
    }


def layer_norm(values):
    mean_val = lax.optimization_barrier(jnp.mean(values, -1, keepdims=True))
    centered = values - mean_val
    variance = lax.optimization_barrier(jnp.mean(centered * centered, -1, keepdims=True))
    return centered * lax.rsqrt(variance + 1e-05)

def reference(hidden_in, segment_ids, page_table, qkv_master, up_master, dense_weight):
    qkv_w = qkv_master.astype(jnp.bfloat16)
    up_w = up_master.astype(jnp.bfloat16)
    slopes = jnp.exp2(-8.0 * (jnp.arange(H) + 1).astype(jnp.float32) / H)
    positions = jnp.arange(TOK_GRP)
    distance = (positions[:, None] - positions[None, :]).astype(jnp.float32)
    dense_blocks = dense_weight.reshape(N_MP, D // N_MP, D).astype(jnp.float32)

    def one_group(inputs):
        tokens, segment, table = inputs
        normed = layer_norm(tokens.astype(jnp.float32)).astype(jnp.bfloat16)
        joined = jnp.dot(normed, qkv_w, preferred_element_type=jnp.float32).astype(jnp.bfloat16)
        joined = joined.reshape(TOK_GRP, H, 3, HD)
        query = joined[:, :, 0].transpose(1, 0, 2)
        keys = joined[:, :, 1].transpose(1, 0, 2)
        vals = joined[:, :, 2].transpose(1, 0, 2)
        allowed = (segment[:, None] == segment[None, :]) & (distance >= 0)

        def one_head(head_in):
            head_query, head_keys, head_vals, slope = head_in
            scores = jnp.dot(head_query, head_keys.T, preferred_element_type=jnp.float32) / jnp.sqrt(jnp.float32(HD))
            scores = jnp.where(allowed, scores - slope * distance, -jnp.inf)
            probs = jax.nn.softmax(scores, axis=-1).astype(jnp.bfloat16)
            return jnp.dot(probs, head_vals, preferred_element_type=jnp.float32).astype(jnp.bfloat16)
        context = lax.map(one_head, (query, keys, vals, slopes))
        context = context.transpose(1, 0, 2).reshape(TOK_GRP, D)
        blocks = context.reshape(TOK_GRP, N_MP, D // N_MP).astype(jnp.float32)
        terms = jnp.einsum('tgc,gce->gte', blocks, dense_blocks)
        terms = lax.optimization_barrier(terms.astype(jnp.bfloat16)).astype(jnp.float32)
        stream = tokens.astype(jnp.float32) + lax.optimization_barrier(jnp.sum(terms, 0))
        normed_two = layer_norm(stream).astype(jnp.bfloat16)
        upper = jnp.dot(normed_two, up_w, preferred_element_type=jnp.float32)
        activated = jax.nn.gelu(upper, approximate=True).astype(jnp.bfloat16)
        key_vals = jnp.stack([joined[:, :, 1], joined[:, :, 2]], 1)
        key_vals = key_vals.reshape(PAGES_GRP, PAGE, 2, H, HD).transpose(0, 2, 3, 1, 4)
        cache = jnp.zeros((PAGES_GRP, 2, H, PAGE, HD), jnp.bfloat16).at[table].set(key_vals)
        return (stream.astype(jnp.bfloat16), activated, cache)
    grouped = hidden_in.reshape(N_DP, TOK_GRP, D)
    hidden_out, activated, cache = lax.map(one_group, (grouped, segment_ids, page_table))
    return (hidden_out.reshape(TOKENS, D), activated.reshape(TOKENS, FF), cache.reshape(PAGES, 2, H, PAGE, HD))
```

```python
import functools

import jax
import jax.numpy as jnp
from jax import lax
from jax.experimental import pallas as pl
from jax.experimental.pallas import tpu as pltpu
from jax.sharding import PartitionSpec as P

H = 16
HD = 128
PAGE = 128
AXES = ("dp", "mp")
BF = jnp.bfloat16
F32 = jnp.float32
VMEM_LIMIT = 48 * 1024 * 1024


def layer_norm(values):
    mean_val = jnp.mean(values, -1, keepdims=True)
    centered = values - mean_val
    variance = jnp.mean(centered * centered, -1, keepdims=True)
    return centered * lax.rsqrt(variance + 1e-05)


def attend(normed, qkv_w, segment, table, mp_index):
    group_rows = normed.shape[0]
    heads_dev = qkv_w.shape[1] // (3 * HD)
    joined = jnp.dot(normed, qkv_w, preferred_element_type=F32).astype(BF)
    joined = joined.reshape(group_rows, heads_dev, 3, HD)
    query = joined[:, :, 0]
    keys = joined[:, :, 1]
    vals = joined[:, :, 2]
    head_ids = mp_index * heads_dev + jnp.arange(heads_dev)
    slopes = jnp.exp2(-8.0 * (head_ids + 1).astype(F32) / H)
    positions = jnp.arange(group_rows)
    distance = (positions[:, None] - positions[None, :]).astype(F32)
    allowed = (segment[:, None] == segment[None, :]) & (distance >= 0)
    scores = jnp.einsum("thd,shd->hts", query, keys, preferred_element_type=F32) / jnp.sqrt(F32(HD))
    scores = scores - slopes[:, None, None] * distance[None]
    scores = jnp.where(allowed[None], scores, -jnp.inf)
    probs = jax.nn.softmax(scores, axis=-1).astype(BF)
    context = jnp.einsum("hts,shd->thd", probs, vals, preferred_element_type=F32).astype(BF)
    context = context.reshape(group_rows, heads_dev * HD)
    key_vals = jnp.stack([keys, vals], 1)
    pages_here = group_rows // PAGE
    key_vals = key_vals.reshape(pages_here, PAGE, 2, heads_dev, HD).transpose(0, 2, 3, 1, 4)
    cache = jnp.zeros((pages_here, 2, heads_dev, PAGE, HD), BF).at[table].set(key_vals)
    return context, cache


def local_any(hidden_in, segment_ids, page_table, qkv_master, up_master, dense_weight):
    mp_index = lax.axis_index("mp")

    def columns(master):
        mine = lax.all_to_all(master.astype(BF), "mp", split_axis=1, concat_axis=0, tiled=True)
        return lax.all_gather(mine, "dp", axis=0, tiled=True)

    qkv_w = columns(qkv_master)
    up_w = columns(up_master)
    normed_own = layer_norm(hidden_in.astype(F32)).astype(BF)
    normed = lax.all_gather(normed_own, "mp", axis=0, tiled=True)
    context, cache = attend(normed, qkv_w, segment_ids[0], page_table[0], mp_index)
    term = jnp.dot(context, dense_weight, preferred_element_type=F32).astype(BF)
    share = lax.psum_scatter(term, "mp", scatter_dimension=0, tiled=True).astype(F32)
    stream_own = hidden_in.astype(F32) + share
    normed_two = lax.all_gather(layer_norm(stream_own).astype(BF), "mp", axis=0, tiled=True)
    upper = jnp.dot(normed_two, up_w, preferred_element_type=F32)
    activated = jax.nn.gelu(upper, approximate=True).astype(BF)
    return stream_own.astype(BF), activated, cache


NZ, NY, NM = 4, 2, 4
PLANE = NY * NM


def pairs(move):
    out = []
    for z in range(NZ):
        for y in range(NY):
            for m in range(NM):
                to = move(z, y, m)
                if to is not None:
                    out.append(((z * NY + y) * NM + m, (to[0] * NY + to[1]) * NM + to[2]))
    return out


CORE = pairs(lambda z, y, m: (z, y, m ^ 1))
XSWAP = pairs(lambda z, y, m: (z, y, m ^ 2))
YSWAP = pairs(lambda z, y, m: (z, y ^ 1, m))
UP = pairs(lambda z, y, m: (z + 1, y, m) if z < NZ - 1 else None)
DOWN = pairs(lambda z, y, m: (z - 1, y, m) if z > 0 else None)
PLANES = [[z * PLANE + i for i in range(PLANE)] for z in range(NZ)]


def send(value, moves):
    return lax.ppermute(value, AXES, moves)


def params(**more):
    return pltpu.CompilerParams(vmem_limit_bytes=VMEM_LIMIT, **more)


ANY = pl.BlockSpec(memory_space=pl.ANY)
SMEM = pl.BlockSpec(memory_space=pltpu.SMEM)
VMEM = pl.BlockSpec(memory_space=pltpu.VMEM)


def cast_kernel(src, dst):
    dst[0] = src[...].astype(BF)


def cast_pieces(master, parts, part):
    rows, cols = master.shape
    width = cols // PLANE // parts

    def place(p):
        return (0, (2 * (p % NM) + p // NM) * parts + part)

    return pl.pallas_call(
        cast_kernel,
        grid=(PLANE,),
        in_specs=[pl.BlockSpec((rows, width), place)],
        out_specs=pl.BlockSpec((1, rows, width), lambda p: (p, 0, 0)),
        out_shape=jax.ShapeDtypeStruct((PLANE, rows, width), BF),
        compiler_params=params(),
    )(master)


def in_plane(pieces):
    return lax.all_to_all(pieces, AXES, split_axis=0, concat_axis=0, tiled=True, axis_index_groups=PLANES)


def ring(mine):
    above, below = [mine], [mine]
    for _ in range(NZ - 1):
        below.append(send(below[-1], UP))
        above.append(send(above[-1], DOWN))
    return [mine] + below[1:] + above[1:]


def load_shards(z, shards, wbuf, sem):
    own, below, above = shards[0], shards[1:NZ], shards[NZ:]
    rows = own.shape[0]

    def start(src, slot):
        pltpu.make_async_copy(src, wbuf.at[pl.ds(slot * rows, rows)], sem.at[slot]).start()

    for slot in range(NZ):
        @pl.when(z == slot)
        def _():
            start(own, slot)

        for far in range(1, NZ):
            if slot + far < NZ:
                @pl.when(z == slot + far)
                def _():
                    start(below[far - 1], slot)

            if slot - far >= 0:
                @pl.when(z == slot - far)
                def _():
                    start(above[far - 1], slot)

    def wait():
        for slot in range(NZ):
            pltpu.make_async_copy(own, wbuf.at[pl.ds(slot * rows, rows)], sem.at[slot]).wait()

    return wait


def head_kernel(pos, slope, seg_rows, seg_cols, normed, *rest):
    shards = rest[: 2 * NZ - 1]
    ctx, kv_own, kv_other, wbuf, sem = rest[2 * NZ - 1 :]
    z, y = pos[0], pos[1]
    wait = load_shards(z, shards, wbuf, sem)
    group = normed.shape[0] // NY
    here = lax.broadcasted_iota(jnp.int32, (group, group), 0)
    there = lax.broadcasted_iota(jnp.int32, (group, group), 1)
    distance = here - there
    fall = slope[0] * distance.astype(F32)
    wait()
    for g, kv in ((0, kv_own), (1, kv_other)):
        first = pl.multiple_of((y ^ g) * group, group)
        rows = pl.ds(first, group)
        joined = jnp.dot(normed[rows, :], wbuf[...], preferred_element_type=F32).astype(BF)
        query, keys, vals = joined[:, :HD], joined[:, HD : 2 * HD], joined[:, 2 * HD :]
        scores = lax.dot_general(query, keys, (((1,), (1,)), ((), ())), preferred_element_type=F32)
        scores = scores * (1.0 / HD**0.5) - fall
        allowed = (seg_cols[g] == seg_rows[g]) & (distance >= 0)
        scores = jnp.where(allowed, scores, -jnp.inf)
        top = jnp.max(scores, -1, keepdims=True)
        raised = jnp.exp(scores - top)
        probs = (raised / jnp.sum(raised, -1, keepdims=True)).astype(BF)
        ctx[rows, :] = jnp.dot(probs, vals, preferred_element_type=F32).astype(BF)
        for b in range(group // PAGE):
            kv[b, 0] = keys[b * PAGE : (b + 1) * PAGE]
            kv[b, 1] = vals[b * PAGE : (b + 1) * PAGE]


def one_head(pos, slope, seg_rows, seg_cols, normed, shards):
    tokens, depth = normed.shape
    width = shards[0].shape[1]
    kv_shape = jax.ShapeDtypeStruct((tokens // NY // PAGE, 2, PAGE, HD), BF)
    return pl.pallas_call(
        head_kernel,
        in_specs=[SMEM, SMEM, VMEM, VMEM, VMEM] + [ANY] * len(shards),
        out_specs=[VMEM, VMEM, VMEM],
        out_shape=[jax.ShapeDtypeStruct((tokens, HD), BF), kv_shape, kv_shape],
        scratch_shapes=[pltpu.VMEM((depth, width), BF), pltpu.SemaphoreType.DMA((NZ,))],
        compiler_params=params(),
        cost_estimate=pl.CostEstimate(
            flops=2 * tokens * depth * width, bytes_accessed=2 * depth * (tokens + width), transcendentals=0
        ),
    )(pos, slope, seg_rows, seg_cols, normed, *shards)


def dense_kernel(pos, hidden, ctx, *rest):
    blocks = rest[:NM]
    out, normed = rest[NM:]
    m = pos[2]
    total = None
    for r in range(NM):
        owner = m ^ r
        left = jnp.concatenate([ctx[owner], ctx[NM + owner]], axis=1)
        term = jnp.dot(left, blocks[r][...], preferred_element_type=F32).astype(BF).astype(F32)
        total = term if total is None else total + term
    stream = hidden[...].astype(F32) + total
    out[...] = stream.astype(BF)
    normed[...] = layer_norm(stream).astype(BF)


def dense_norm(pos, hidden, ctx, blocks):
    shape = jax.ShapeDtypeStruct(hidden.shape, BF)
    return pl.pallas_call(
        dense_kernel,
        in_specs=[SMEM, VMEM, VMEM] + [VMEM] * NM,
        out_specs=[VMEM, VMEM],
        out_shape=[shape, shape],
        compiler_params=params(),
    )(pos, hidden, ctx, *blocks)


def up_kernel(pos, *rest):
    pieces = rest[:10]
    shards = rest[10 : 10 + 2 * NZ - 1]
    act_own, act_other, xbuf, wbuf, xsem, sem = rest[10 + 2 * NZ - 1 :]
    z, m = pos[0], pos[2]
    wait = load_shards(z, shards, wbuf, sem)
    group = act_own.shape[0]
    share = group // NM
    half = share // 2
    place = [(0, 0, 0), (0, 1, 0), (0, 2, 0), (0, 3, 0), (1, 0, 0), (1, 1, 0)]
    place += [(1, 2, 0), (1, 2, half), (1, 3, 0), (1, 3, half)]
    copies = []
    for i, (g, r, extra) in enumerate(place):
        first = pl.multiple_of(g * group + (m ^ r) * share + extra, 16)
        copies.append(pltpu.make_async_copy(pieces[i], xbuf.at[pl.ds(first, pieces[i].shape[0])], xsem.at[i]))
    for copy in copies:
        copy.start()
    for copy in copies:
        copy.wait()
    wait()
    for g, act in ((1, act_other), (0, act_own)):
        upper = jnp.dot(xbuf[g * group : (g + 1) * group], wbuf[...], preferred_element_type=F32)
        act[...] = jax.nn.gelu(upper, approximate=True).astype(BF)


def up_part(pos, pieces, shards):
    group = pieces[0].shape[0] * NM
    depth, width = pieces[0].shape[1], shards[0].shape[1]
    shape = jax.ShapeDtypeStruct((group, width), BF)
    return pl.pallas_call(
        up_kernel,
        in_specs=[SMEM] + [ANY] * (10 + len(shards)),
        out_specs=[VMEM, VMEM],
        out_shape=[shape, shape],
        scratch_shapes=[
            pltpu.VMEM((NY * group, depth), BF),
            pltpu.VMEM((depth, width), BF),
            pltpu.SemaphoreType.DMA((10,)),
            pltpu.SemaphoreType.DMA((NZ,)),
        ],
        compiler_params=params(),
        cost_estimate=pl.CostEstimate(
            flops=4 * group * depth * width, bytes_accessed=2 * depth * (2 * group + width), transcendentals=0
        ),
    )(pos, *pieces, *shards)


def join_kernel(pos, *rest):
    *parts, out = rest
    y = pos[1]
    count = len(parts) // 2
    width = parts[0].shape[1]
    for side in range(2):
        for j in range(count):
            first = pl.multiple_of((y ^ side) * (count * width) + j * width, width)
            out[:, pl.ds(first, width)] = parts[side * count + j][...]


def join_columns(pos, own, got):
    group, width = own[0].shape
    return pl.pallas_call(
        join_kernel,
        in_specs=[SMEM] + [VMEM] * (len(own) + len(got)),
        out_specs=VMEM,
        out_shape=jax.ShapeDtypeStruct((group, width * (len(own) + len(got))), BF),
        compiler_params=params(),
    )(pos, *own, *got)


def pages_kernel(pos, table, *rest):
    *parts, out = rest
    y = pos[1]
    for b in range(parts[0].shape[0]):
        slot = table[0, b]
        for side in range(2):
            for h in range(2):
                out[slot, :, (y ^ side) * 2 + h] = parts[side * 2 + h][b]


def place_pages(pos, table, own, got):
    blocks, two, page, width = own[0].shape
    return pl.pallas_call(
        pages_kernel,
        in_specs=[SMEM, SMEM] + [VMEM] * 4,
        out_specs=VMEM,
        out_shape=jax.ShapeDtypeStruct((blocks, two, 4, page, width), BF),
        compiler_params=params(),
    )(pos, table, *own, *got)


def gather_plane(mine):
    half = mine.shape[0] // 2
    from_y = send(mine, YSWAP)
    from_x = send(mine, XSWAP)
    far_low = send(from_y[:half], XSWAP)
    far_high = send(from_x[half:], YSWAP)
    other = [send(v, CORE) for v in (mine, from_y, from_x, far_low, far_high)]
    return [mine, other[0], from_x, other[2], from_y, other[1], far_low, far_high, other[3], other[4]]


def local_planes(hidden_in, segment_ids, page_table, qkv_master, up_master, dense_weight):
    dp, mp = lax.axis_index("dp"), lax.axis_index("mp")
    z, y = dp // NY, dp % NY
    pos = jnp.stack([z, y, mp]).astype(jnp.int32)

    heads = 2
    pieces = cast_pieces(qkv_master, 1, 0)
    swapped = in_plane(pieces)
    q_shards = []
    for h in range(heads):
        width = swapped.shape[2] // heads
        q_shards.append(swapped[:, :, h * width : (h + 1) * width].reshape(-1, width))

    parts = 2
    up_pieces = [cast_pieces(up_master, parts, j) for j in range(parts)]
    up_shards = [in_plane(p) for p in up_pieces]
    up_shards = [s.reshape(-1, s.shape[2]) for s in up_shards]

    normed_own = layer_norm(hidden_in.astype(F32)).astype(BF)
    normed = lax.all_gather(normed_own, AXES, axis=0, tiled=True, axis_index_groups=PLANES)
    segments = jnp.concatenate([segment_ids, send(segment_ids, YSWAP)], 0)
    seg_rows, seg_cols = segments[:, None, :], segments[:, :, None]

    q_rings = [ring(s) for s in q_shards]

    dense_x = send(dense_weight, XSWAP)
    dense_c = send(dense_weight, CORE)
    dense_xc = send(dense_x, CORE)

    contexts, kv_own, kv_got = [], [], []
    for h in range(heads):
        head = 4 * mp + 2 * y + h
        slope = jnp.exp2(-8.0 * (head + 1).astype(F32) / H).reshape(1)
        ctx, own, other = one_head(pos, slope, seg_rows, seg_cols, normed, q_rings[h])
        contexts.append(ctx)
        kv_own.append(own)
        kv_got.append(send(other, YSWAP))
    context = jnp.concatenate(contexts, 1).reshape(PLANE, -1, heads * HD)
    ctx_own = in_plane(context)
    hidden_out, normed_two = dense_norm(
        pos, hidden_in, ctx_own, [dense_weight, dense_c, dense_x, dense_xc]
    )
    tokens = gather_plane(normed_two)

    up_rings = [ring(s) for s in up_shards]
    act_own, act_got = [], []
    for j in range(parts):
        own, other = up_part(pos, tokens, up_rings[j])
        act_own.append(own)
        act_got.append(send(other, YSWAP))
    activated = join_columns(pos, act_own, act_got)
    cache = place_pages(pos, page_table, kv_own, kv_got)
    return hidden_out, activated, cache


def solution(mesh):
    placed = (
        P(("dp", "mp"), None),
        P("dp", None),
        P("dp", None),
        P(("dp", "mp"), None),
        P(("dp", "mp"), None),
        P("mp", None),
    )
    planes = mesh.shape["dp"] == NZ * NY and mesh.shape["mp"] == NM
    return jax.shard_map(
        local_planes if planes else local_any,
        mesh=mesh,
        in_specs=placed,
        out_specs=(P(("dp", "mp"), None), P("dp", "mp"), P("dp", None, "mp", None, None)),
        check_vma=False,
    )
```

```python
import functools

import jax
import jax.numpy as jnp
from jax import lax
from jax.experimental import pallas as pl
from jax.experimental.pallas import tpu as pltpu
from jax.sharding import PartitionSpec as P

H = 16
HD = 128
PAGE = 128
AXES = ("dp", "mp")
BF = jnp.bfloat16
F32 = jnp.float32
VMEM_LIMIT = 56 * 1024 * 1024


def layer_norm(values):
    mean_val = jnp.mean(values, -1, keepdims=True)
    centered = values - mean_val
    variance = jnp.mean(centered * centered, -1, keepdims=True)
    return centered * lax.rsqrt(variance + 1e-05)


def attend(normed, qkv_w, segment, table, mp_index):
    group_rows = normed.shape[0]
    heads_dev = qkv_w.shape[1] // (3 * HD)
    joined = jnp.dot(normed, qkv_w, preferred_element_type=F32).astype(BF)
    joined = joined.reshape(group_rows, heads_dev, 3, HD)
    query = joined[:, :, 0]
    keys = joined[:, :, 1]
    vals = joined[:, :, 2]
    head_ids = mp_index * heads_dev + jnp.arange(heads_dev)
    slopes = jnp.exp2(-8.0 * (head_ids + 1).astype(F32) / H)
    positions = jnp.arange(group_rows)
    distance = (positions[:, None] - positions[None, :]).astype(F32)
    allowed = (segment[:, None] == segment[None, :]) & (distance >= 0)
    scores = jnp.einsum("thd,shd->hts", query, keys, preferred_element_type=F32) / jnp.sqrt(F32(HD))
    scores = scores - slopes[:, None, None] * distance[None]
    scores = jnp.where(allowed[None], scores, -jnp.inf)
    probs = jax.nn.softmax(scores, axis=-1).astype(BF)
    context = jnp.einsum("hts,shd->thd", probs, vals, preferred_element_type=F32).astype(BF)
    context = context.reshape(group_rows, heads_dev * HD)
    key_vals = jnp.stack([keys, vals], 1)
    pages_here = group_rows // PAGE
    key_vals = key_vals.reshape(pages_here, PAGE, 2, heads_dev, HD).transpose(0, 2, 3, 1, 4)
    cache = jnp.zeros((pages_here, 2, heads_dev, PAGE, HD), BF).at[table].set(key_vals)
    return context, cache


def local_any(hidden_in, segment_ids, page_table, qkv_master, up_master, dense_weight):
    mp_index = lax.axis_index("mp")

    def columns(master):
        mine = lax.all_to_all(master.astype(BF), "mp", split_axis=1, concat_axis=0, tiled=True)
        return lax.all_gather(mine, "dp", axis=0, tiled=True)

    qkv_w = columns(qkv_master)
    up_w = columns(up_master)
    normed_own = layer_norm(hidden_in.astype(F32)).astype(BF)
    normed = lax.all_gather(normed_own, "mp", axis=0, tiled=True)
    context, cache = attend(normed, qkv_w, segment_ids[0], page_table[0], mp_index)
    term = jnp.dot(context, dense_weight, preferred_element_type=F32).astype(BF)
    share = lax.psum_scatter(term, "mp", scatter_dimension=0, tiled=True).astype(F32)
    stream_own = hidden_in.astype(F32) + share
    normed_two = lax.all_gather(layer_norm(stream_own).astype(BF), "mp", axis=0, tiled=True)
    upper = jnp.dot(normed_two, up_w, preferred_element_type=F32)
    activated = jax.nn.gelu(upper, approximate=True).astype(BF)
    return stream_own.astype(BF), activated, cache


NZ, NY, NM = 4, 2, 4
PLANE = NY * NM
HEADS = H // PLANE


def pairs(move):
    out = []
    for z in range(NZ):
        for y in range(NY):
            for m in range(NM):
                to = move(z, y, m)
                if to is not None:
                    out.append(((z * NY + y) * NM + m, (to[0] * NY + to[1]) * NM + to[2]))
    return out


CORE = pairs(lambda z, y, m: (z, y, m ^ 1))
XSWAP = pairs(lambda z, y, m: (z, y, m ^ 2))
YSWAP = pairs(lambda z, y, m: (z, y ^ 1, m))
ZSWAP = pairs(lambda z, y, m: (z ^ 1, y, m))
PLANES = [[z * PLANE + i for i in range(PLANE)] for z in range(NZ)]
QUADS = [[z * PLANE + 2 * i + c for i in range(PLANE // 2)] for z in range(NZ) for c in range(2)]


def send(value, moves):
    return lax.ppermute(value, AXES, moves)


def window(*values):
    return lax.optimization_barrier(values)


def params(**more):
    return pltpu.CompilerParams(vmem_limit_bytes=VMEM_LIMIT, **more)


ANY = pl.BlockSpec(memory_space=pltpu.HBM)
SMEM = pl.BlockSpec(memory_space=pltpu.SMEM)
VMEM = pl.BlockSpec(memory_space=pltpu.VMEM)


def cast_pieces(master):
    rows, cols = master.shape
    width = cols // PLANE // 2

    def kernel(src, dst):
        for p in range(PLANE):
            for part in range(2):
                start = ((2 * (p % NM) + p // NM) * 2 + part) * width
                piece = src[:, start : start + width].astype(BF)
                for z in range(part, NZ, 2):
                    dst[z * PLANE + p] = piece

    return pl.pallas_call(
        kernel,
        in_specs=[VMEM],
        out_specs=VMEM,
        out_shape=jax.ShapeDtypeStruct((NZ * PLANE, rows, width), BF),
        compiler_params=params(),
    )(master)


def pack_kernel(*refs):
    *parts, out = refs
    at = 0
    for part in parts:
        out[at : at + part.shape[0]] = part[...]
        at += part.shape[0]


def pack_rows(*parts):
    rows = sum(part.shape[0] for part in parts)
    return pl.pallas_call(
        pack_kernel,
        in_specs=[VMEM] * len(parts),
        out_specs=VMEM,
        out_shape=jax.ShapeDtypeStruct((rows, parts[0].shape[1]), BF),
        compiler_params=params(),
    )(*parts)


def norm_kernel(hidden, out):
    out[...] = layer_norm(hidden[...].astype(F32)).astype(BF)


def norm_rows(hidden):
    return pl.pallas_call(
        norm_kernel,
        in_specs=[VMEM],
        out_specs=VMEM,
        out_shape=jax.ShapeDtypeStruct(hidden.shape, BF),
        compiler_params=params(),
    )(hidden)


def to_all(pieces):
    mine = lax.all_to_all(pieces, AXES, split_axis=0, concat_axis=0, tiled=True)
    return mine.reshape(-1, mine.shape[2])


def in_plane(pieces):
    return lax.all_to_all(pieces, AXES, split_axis=0, concat_axis=0, tiled=True, axis_index_groups=PLANES)


def token_copies(y, m, mine, other, xbuf, sem):
    share = mine.shape[0] // NM
    half = share // 2
    place = [(0, 0, 0, share), (1, 0, 0, share), (0, 2, 0, share), (1, 2, 0, half), (1, 2, half, half)]
    copies = []
    for side, src in ((0, mine), (1, other)):
        at = 0
        for dy, dm, extra, rows in place:
            first = pl.multiple_of(((y ^ dy) * NM + (m ^ dm ^ side)) * share + extra, 16)
            copies.append(
                pltpu.make_async_copy(
                    src.at[pl.ds(at, rows)], xbuf.at[pl.ds(first, rows)], sem.at[len(copies)]
                )
            )
            at += rows
    return copies


TOKEN_COPIES = 10


def head_kernel(pos, slope, seg_rows, seg_cols, mine, other, w_own, w_got, ctx, kv_own, kv_other, xbuf, wbuf, xsem, wsem):
    z, y, m = pos[0], pos[1], pos[2]
    copies = [
        pltpu.make_async_copy(w_own, wbuf.at[z % 2], wsem.at[0]),
        pltpu.make_async_copy(w_got, wbuf.at[1 - z % 2], wsem.at[1]),
    ] + token_copies(y, m, mine, other, xbuf, xsem)
    for copy in copies:
        copy.start()
    group = xbuf.shape[0] // NY
    here = lax.broadcasted_iota(jnp.int32, (group, group), 0)
    there = lax.broadcasted_iota(jnp.int32, (group, group), 1)
    distance = here - there
    away = distance.astype(F32)
    for copy in copies:
        copy.wait()
    for g, kv in ((0, kv_own), (1, kv_other)):
        first = pl.multiple_of((y ^ g) * group, group)
        rows = pl.ds(first, group)
        allowed = (seg_cols[g] == seg_rows[g]) & (distance >= 0)
        for h in range(HEADS):
            joined = jnp.dot(xbuf[rows, :], wbuf[h], preferred_element_type=F32).astype(BF)
            query, keys, vals = (joined[:, i * HD : (i + 1) * HD] for i in range(3))
            scores = lax.dot_general(query, keys, (((1,), (1,)), ((), ())), preferred_element_type=F32)
            scores = scores * (1.0 / HD**0.5) - slope[h] * away
            scores = jnp.where(allowed, scores, -jnp.inf)
            top = jnp.max(scores, -1, keepdims=True)
            raised = jnp.exp(scores - top)
            probs = (raised / jnp.sum(raised, -1, keepdims=True)).astype(BF)
            ctx[rows, h * HD : (h + 1) * HD] = jnp.dot(probs, vals, preferred_element_type=F32).astype(BF)
            for b in range(group // PAGE):
                kv[b, 0, h] = keys[b * PAGE : (b + 1) * PAGE]
                kv[b, 1, h] = vals[b * PAGE : (b + 1) * PAGE]


def two_heads(pos, slope, seg_rows, seg_cols, tokens, w_own, w_got):
    count, depth = 2 * tokens[0].shape[0], tokens[0].shape[1]
    width = w_own.shape[1]
    kv_shape = jax.ShapeDtypeStruct((count // NY // PAGE, 2, HEADS, PAGE, HD), BF)
    return pl.pallas_call(
        head_kernel,
        in_specs=[SMEM, SMEM, VMEM, VMEM] + [ANY] * 4,
        out_specs=[VMEM, VMEM, VMEM],
        out_shape=[jax.ShapeDtypeStruct((count, HEADS * HD), BF), kv_shape, kv_shape],
        scratch_shapes=[
            pltpu.VMEM((count, depth), BF),
            pltpu.VMEM((HEADS, depth, width), BF),
            pltpu.SemaphoreType.DMA((TOKEN_COPIES,)),
            pltpu.SemaphoreType.DMA((2,)),
        ],
        compiler_params=params(),
    )(pos, slope, seg_rows, seg_cols, *tokens, w_own, w_got)


def dense_kernel(pos, hidden, ctx, *rest):
    blocks = rest[:NM]
    out, normed = rest[NM:]
    y, m = pos[1], pos[2]
    half = blocks[0].shape[0] // 2
    total = None
    for r in range(NM):
        owner = m ^ r
        flip = y if r >= 2 else 0
        near = jnp.dot(ctx[flip * NM + owner], blocks[r][:half], preferred_element_type=F32)
        far = jnp.dot(ctx[(flip ^ 1) * NM + owner], blocks[r][half:], preferred_element_type=F32)
        term = (near + far).astype(BF).astype(F32)
        total = term if total is None else total + term
    stream = hidden[...].astype(F32) + total
    out[...] = stream.astype(BF)
    normed[...] = layer_norm(stream).astype(BF)


def dense_norm(pos, hidden, ctx, blocks):
    return pl.pallas_call(
        dense_kernel,
        in_specs=[SMEM] + [VMEM] * (2 + len(blocks)),
        out_specs=[VMEM, VMEM],
        out_shape=[jax.ShapeDtypeStruct(hidden.shape, BF)] * 2,
        compiler_params=params(),
    )(pos, hidden, ctx, *blocks)


def up_kernel(count, *refs):
    pieces, weights = refs[:count], refs[count : (len(refs) - 2 + count) // 2]
    acts, xbuf, sem = refs[count + len(weights) : -2], refs[-2], refs[-1]
    copies = []
    at = 0
    for i, piece in enumerate(pieces):
        rows = piece.shape[0]
        copies.append(pltpu.make_async_copy(piece, xbuf.at[at : at + rows], sem.at[i]))
        at += rows
    for copy in copies:
        copy.start()
    for copy in copies:
        copy.wait()
    for w, act in zip(weights, acts):
        upper = jnp.dot(xbuf[...], w[...], preferred_element_type=F32)
        act[...] = jax.nn.gelu(upper, approximate=True).astype(BF)


def up_part(pieces, weights):
    rows, depth = sum(piece.shape[0] for piece in pieces), pieces[0].shape[1]
    return pl.pallas_call(
        functools.partial(up_kernel, len(pieces)),
        in_specs=[ANY] * len(pieces) + [VMEM] * len(weights),
        out_specs=[VMEM] * len(weights),
        out_shape=[jax.ShapeDtypeStruct((rows, w.shape[1]), BF) for w in weights],
        scratch_shapes=[pltpu.VMEM((rows, depth), BF), pltpu.SemaphoreType.DMA((len(pieces),))],
        compiler_params=params(),
    )(*pieces, *weights)


def join_kernel(pos, own_a, own_b, got_a, got_b, out):
    z, y, m = pos[0], pos[1], pos[2]
    width = own_a.shape[1]
    share = out.shape[0] // NM
    for side, parts in ((0, (own_a, own_b)), (1, (got_a, got_b))):
        for j, part in enumerate(parts):
            first = ((y ^ side) * 2 + (z % 2 + j) % 2) * width
            for i, r in enumerate((0, 2, 1, 3)):
                rows = pl.ds(pl.multiple_of((m ^ r) * share, 16), share)
                out[rows, pl.ds(pl.multiple_of(first, width), width)] = part[i * share : (i + 1) * share]


def join_parts(pos, *parts):
    rows, width = parts[0].shape
    return pl.pallas_call(
        join_kernel,
        in_specs=[SMEM] + [VMEM] * 4,
        out_specs=VMEM,
        out_shape=jax.ShapeDtypeStruct((rows, 4 * width), BF),
        compiler_params=params(),
    )(pos, *parts)


def pages_kernel(pos, table, own, got, out):
    y = pos[1]
    for b in range(own.shape[0]):
        slot = table[0, b]
        for side, part in ((0, own), (1, got)):
            for h in range(HEADS):
                out[slot, :, (y ^ side) * HEADS + h] = part[b, :, h]


def place_pages(pos, table, own, got):
    blocks, two, heads, page, width = own.shape
    return pl.pallas_call(
        pages_kernel,
        in_specs=[SMEM, SMEM, VMEM, VMEM],
        out_specs=VMEM,
        out_shape=jax.ShapeDtypeStruct((blocks, two, NY * heads, page, width), BF),
        compiler_params=params(),
    )(pos, table, own, got)


def in_quad(copies):
    return lax.all_to_all(copies, AXES, split_axis=0, concat_axis=0, tiled=True, axis_index_groups=QUADS)


def local_planes(hidden_in, segment_ids, page_table, qkv_master, up_master, dense_weight):
    dp, mp = lax.axis_index("dp"), lax.axis_index("mp")
    z, y = dp // NY, dp % NY
    pos = jnp.stack([z, y, mp]).astype(jnp.int32)
    half = dense_weight.shape[0] // 2
    share = hidden_in.shape[0]
    head = H // NM * mp + HEADS * y + jnp.arange(HEADS)
    slopes = jnp.exp2(-8.0 * (head + 1).astype(F32) / H)

    qkv_own = to_all(cast_pieces(qkv_master))
    normed = norm_rows(hidden_in)
    from_y = send(normed, YSWAP)
    from_x = send(normed, XSWAP)
    cross_low = send(from_y[: share // 2], XSWAP)
    cross_high = send(from_x[share // 2 :], YSWAP)
    mine = pack_rows(normed, from_y, from_x, cross_low, cross_high)
    up_pieces = cast_pieces(up_master)
    give = lax.dynamic_slice_in_dim(dense_weight, y * half, half, 0)
    seg_other = send(segment_ids, YSWAP)
    qkv_own, mine, up_pieces, give, seg_other, dense_own, segment_ids = window(
        qkv_own, mine, up_pieces, give, seg_other, dense_weight, segment_ids
    )

    up_own = to_all(up_pieces)
    qkv_got = send(qkv_own, ZSWAP)
    other = send(mine, CORE)
    near = send(give, XSWAP)
    far = send(near, YSWAP)
    dense_c = send(dense_own, CORE)
    segments = jnp.concatenate([segment_ids, seg_other], 0)
    seg_rows, seg_cols = segments[:, None, :], segments[:, :, None]
    context, kv_own, kv_other = two_heads(pos, slopes, seg_rows, seg_cols, (mine, other), qkv_own, qkv_got)
    up_own, context, far, near, dense_own, dense_c, kv_own, kv_other = window(
        up_own, context, far, near, dense_own, dense_c, kv_own, kv_other
    )

    up_got = send(up_own, ZSWAP)
    dense_x = pack_rows(near, far)
    dense_xc = send(dense_x, CORE)
    ctx_own = in_plane(context.reshape(PLANE, -1, HEADS * HD))
    hidden_out, normed = dense_norm(pos, hidden_in, ctx_own, [dense_own, dense_c, dense_x, dense_xc])
    from_y = send(normed, YSWAP)
    from_x = send(normed, XSWAP)
    cross_low = send(from_y[: share // 2], XSWAP)
    cross_high = send(from_x[share // 2 :], YSWAP)
    group_own = [normed, from_x]
    group_other = [from_y, cross_low, cross_high]
    group_own += [send(piece, CORE) for piece in group_own]
    group_other += [send(piece, CORE) for piece in group_other]
    up_own, up_got, kv_own, kv_other, *tokens = window(up_own, up_got, kv_own, kv_other, *group_own, *group_other)
    group_own, group_other = tokens[:4], tokens[4:]

    weights = [up_own, up_got]
    act_got = [send(up_part(group_other, [w])[0], YSWAP) for w in weights]
    act_own = up_part(group_own, weights)
    kv_got = send(kv_other, YSWAP)
    activated = join_parts(pos, *act_own, *act_got)
    cache = place_pages(pos, page_table, kv_own, kv_got)
    return hidden_out, activated, cache


def solution(mesh):
    placed = (
        P(("dp", "mp"), None),
        P("dp", None),
        P("dp", None),
        P(("dp", "mp"), None),
        P(("dp", "mp"), None),
        P("mp", None),
    )
    planes = mesh.shape["dp"] == NZ * NY and mesh.shape["mp"] == NM
    return jax.shard_map(
        local_planes if planes else local_any,
        mesh=mesh,
        in_specs=placed,
        out_specs=(P(("dp", "mp"), None), P("dp", "mp"), P("dp", None, "mp", None, None)),
        check_vma=False,
    )
```

```python
import functools

import jax
import jax.numpy as jnp
from jax import lax
from jax.experimental import pallas as pl
from jax.experimental.pallas import tpu as pltpu
from jax.sharding import PartitionSpec as P

H = 16
HD = 128
PAGE = 128
AXES = ("dp", "mp")
BF = jnp.bfloat16
F32 = jnp.float32
VMEM_LIMIT = 56 * 1024 * 1024


def layer_norm(values):
    mean_val = jnp.mean(values, -1, keepdims=True)
    centered = values - mean_val
    variance = jnp.mean(centered * centered, -1, keepdims=True)
    return centered * lax.rsqrt(variance + 1e-05)


def attend(normed, qkv_w, segment, table, mp_index):
    group_rows = normed.shape[0]
    heads_dev = qkv_w.shape[1] // (3 * HD)
    joined = jnp.dot(normed, qkv_w, preferred_element_type=F32).astype(BF)
    joined = joined.reshape(group_rows, heads_dev, 3, HD)
    query = joined[:, :, 0]
    keys = joined[:, :, 1]
    vals = joined[:, :, 2]
    head_ids = mp_index * heads_dev + jnp.arange(heads_dev)
    slopes = jnp.exp2(-8.0 * (head_ids + 1).astype(F32) / H)
    positions = jnp.arange(group_rows)
    distance = (positions[:, None] - positions[None, :]).astype(F32)
    allowed = (segment[:, None] == segment[None, :]) & (distance >= 0)
    scores = jnp.einsum("thd,shd->hts", query, keys, preferred_element_type=F32) / jnp.sqrt(F32(HD))
    scores = scores - slopes[:, None, None] * distance[None]
    scores = jnp.where(allowed[None], scores, -jnp.inf)
    probs = jax.nn.softmax(scores, axis=-1).astype(BF)
    context = jnp.einsum("hts,shd->thd", probs, vals, preferred_element_type=F32).astype(BF)
    context = context.reshape(group_rows, heads_dev * HD)
    key_vals = jnp.stack([keys, vals], 1)
    pages_here = group_rows // PAGE
    key_vals = key_vals.reshape(pages_here, PAGE, 2, heads_dev, HD).transpose(0, 2, 3, 1, 4)
    cache = jnp.zeros((pages_here, 2, heads_dev, PAGE, HD), BF).at[table].set(key_vals)
    return context, cache


def local_any(hidden_in, segment_ids, page_table, qkv_master, up_master, dense_weight):
    mp_index = lax.axis_index("mp")

    def columns(master):
        mine = lax.all_to_all(master.astype(BF), "mp", split_axis=1, concat_axis=0, tiled=True)
        return lax.all_gather(mine, "dp", axis=0, tiled=True)

    qkv_w = columns(qkv_master)
    up_w = columns(up_master)
    normed_own = layer_norm(hidden_in.astype(F32)).astype(BF)
    normed = lax.all_gather(normed_own, "mp", axis=0, tiled=True)
    context, cache = attend(normed, qkv_w, segment_ids[0], page_table[0], mp_index)
    term = jnp.dot(context, dense_weight, preferred_element_type=F32).astype(BF)
    share = lax.psum_scatter(term, "mp", scatter_dimension=0, tiled=True).astype(F32)
    stream_own = hidden_in.astype(F32) + share
    normed_two = lax.all_gather(layer_norm(stream_own).astype(BF), "mp", axis=0, tiled=True)
    upper = jnp.dot(normed_two, up_w, preferred_element_type=F32)
    activated = jax.nn.gelu(upper, approximate=True).astype(BF)
    return stream_own.astype(BF), activated, cache


NZ, NY, NM = 4, 2, 4
PLANE = NY * NM
HEADS = H // PLANE


def pairs(move):
    out = []
    for z in range(NZ):
        for y in range(NY):
            for m in range(NM):
                to = move(z, y, m)
                if to is not None:
                    out.append(((z * NY + y) * NM + m, (to[0] * NY + to[1]) * NM + to[2]))
    return out


CORE = pairs(lambda z, y, m: (z, y, m ^ 1))
XSWAP = pairs(lambda z, y, m: (z, y, m ^ 2))
YSWAP = pairs(lambda z, y, m: (z, y ^ 1, m))
ZSWAP = pairs(lambda z, y, m: (z ^ 1, y, m))
ZFAR = pairs(lambda z, y, m: (z ^ 2, y, m))
PLANES = [[z * PLANE + i for i in range(PLANE)] for z in range(NZ)]
QUADS = [[z * PLANE + 2 * i + c for i in range(PLANE // 2)] for z in range(NZ) for c in range(2)]


def send(value, moves):
    return lax.ppermute(value, AXES, moves)


def window(*values):
    return lax.optimization_barrier(values)


def params(**more):
    return pltpu.CompilerParams(vmem_limit_bytes=VMEM_LIMIT, **more)


HBM = pl.BlockSpec(memory_space=pltpu.HBM)
ANY = pl.BlockSpec(memory_space=pl.ANY)
SMEM = pl.BlockSpec(memory_space=pltpu.SMEM)
VMEM = pl.BlockSpec(memory_space=pltpu.VMEM)


def cast_pieces(master):
    rows, cols = master.shape
    width = cols // PLANE // 2

    def kernel(src, dst):
        for p in range(PLANE):
            for part in range(2):
                start = ((2 * (p % NM) + p // NM) * 2 + part) * width
                piece = src[:, start : start + width].astype(BF)
                for z in range(part, NZ, 2):
                    dst[z * PLANE + p] = piece

    return pl.pallas_call(
        kernel,
        in_specs=[VMEM],
        out_specs=VMEM,
        out_shape=jax.ShapeDtypeStruct((NZ * PLANE, rows, width), BF),
        compiler_params=params(),
    )(master)


def cast_halves(pos, master):
    rows, cols = master.shape
    half = cols // PLANE // 2

    def kernel(pos, src, *dst):
        parity = pos[0] % 2
        for p in range(PLANE):
            start = (2 * (p % NM) + p // NM) * 2 * half
            for i in range(2):
                first = pl.multiple_of(start + (parity ^ i) * half, half)
                dst[i][p] = src[:, pl.ds(first, half)].astype(BF)

    shape = jax.ShapeDtypeStruct((PLANE, rows, half), BF)
    return pl.pallas_call(
        kernel,
        in_specs=[SMEM, VMEM],
        out_specs=[VMEM, VMEM],
        out_shape=[shape, shape],
        compiler_params=params(),
    )(pos, master)


def stack_kernel(own, got, out):
    rows = own.shape[1]
    out[:, :rows] = own[...]
    out[:, rows:] = got[...]


def stack_rows(own, got):
    count, rows, width = own.shape
    return pl.pallas_call(
        stack_kernel,
        in_specs=[VMEM, VMEM],
        out_specs=VMEM,
        out_shape=jax.ShapeDtypeStruct((count, 2 * rows, width), BF),
        compiler_params=params(),
    )(own, got)


def pack_kernel(*refs):
    *parts, out = refs
    at = 0
    for part in parts:
        out[at : at + part.shape[0]] = part[...]
        at += part.shape[0]


def pack_rows(*parts):
    rows = sum(part.shape[0] for part in parts)
    return pl.pallas_call(
        pack_kernel,
        in_specs=[VMEM] * len(parts),
        out_specs=VMEM,
        out_shape=jax.ShapeDtypeStruct((rows, parts[0].shape[1]), BF),
        compiler_params=params(),
    )(*parts)


def norm_kernel(hidden, out):
    out[...] = layer_norm(hidden[...].astype(F32)).astype(BF)


def norm_rows(hidden):
    return pl.pallas_call(
        norm_kernel,
        in_specs=[VMEM],
        out_specs=VMEM,
        out_shape=jax.ShapeDtypeStruct(hidden.shape, BF),
        compiler_params=params(),
    )(hidden)


def to_all(pieces):
    mine = lax.all_to_all(pieces, AXES, split_axis=0, concat_axis=0, tiled=True)
    return mine.reshape(-1, mine.shape[2])


def in_plane(pieces):
    return lax.all_to_all(pieces, AXES, split_axis=0, concat_axis=0, tiled=True, axis_index_groups=PLANES)


def token_copies(y, m, mine, other, xbuf, sem):
    share = mine.shape[0] // NM
    half = share // 2
    place = [(0, 0, 0, share), (1, 0, 0, share), (0, 2, 0, share), (1, 2, 0, half), (1, 2, half, half)]
    copies = []
    for side, src in ((0, mine), (1, other)):
        at = 0
        for dy, dm, extra, rows in place:
            first = pl.multiple_of(((y ^ dy) * NM + (m ^ dm ^ side)) * share + extra, 16)
            copies.append(
                pltpu.make_async_copy(
                    src.at[pl.ds(at, rows)], xbuf.at[pl.ds(first, rows)], sem.at[len(copies)]
                )
            )
            at += rows
    return copies


TOKEN_COPIES = 10


def head_kernel(pos, slope, seg_rows, seg_cols, mine, other, w_own, w_got, ctx, kv_own, kv_other, xbuf, wbuf, xsem, wsem):
    z, y, m = pos[0], pos[1], pos[2]
    width = w_own.shape[1]
    copies = [
        pltpu.make_async_copy(
            src, wbuf.at[:, pl.ds(pl.multiple_of((z % 2 ^ i) * width, width), width)], wsem.at[i]
        )
        for i, src in enumerate((w_own, w_got))
    ] + token_copies(y, m, mine, other, xbuf, xsem)
    for copy in copies:
        copy.start()
    group = xbuf.shape[0] // NY
    here = lax.broadcasted_iota(jnp.int32, (group, group), 0)
    there = lax.broadcasted_iota(jnp.int32, (group, group), 1)
    distance = here - there
    away = distance.astype(F32)
    for copy in copies:
        copy.wait()
    for g, kv in ((0, kv_own), (1, kv_other)):
        first = pl.multiple_of((y ^ g) * group, group)
        rows = pl.ds(first, group)
        allowed = (seg_cols[g] == seg_rows[g]) & (distance >= 0)
        joined = jnp.dot(xbuf[rows, :], wbuf[...], preferred_element_type=F32).astype(BF)
        for h in range(HEADS):
            query, keys, vals = (joined[:, (3 * h + i) * HD : (3 * h + i + 1) * HD] for i in range(3))
            scores = lax.dot_general(query, keys, (((1,), (1,)), ((), ())), preferred_element_type=F32)
            scores = scores * (1.0 / HD**0.5) - slope[h] * away
            scores = jnp.where(allowed, scores, -jnp.inf)
            raised = jnp.exp(scores - jnp.max(scores, -1, keepdims=True))
            probs = (raised * (1.0 / jnp.sum(raised, -1, keepdims=True))).astype(BF)
            ctx[rows, h * HD : (h + 1) * HD] = jnp.dot(probs, vals, preferred_element_type=F32).astype(BF)
            for b in range(group // PAGE):
                kv[b, 0, h] = keys[b * PAGE : (b + 1) * PAGE]
                kv[b, 1, h] = vals[b * PAGE : (b + 1) * PAGE]


def two_heads(pos, slope, seg_rows, seg_cols, tokens, w_own, w_got):
    count, depth = 2 * tokens[0].shape[0], tokens[0].shape[1]
    width = w_own.shape[1]
    kv_shape = jax.ShapeDtypeStruct((count // NY // PAGE, 2, HEADS, PAGE, HD), BF)
    return pl.pallas_call(
        head_kernel,
        in_specs=[SMEM, SMEM, VMEM, VMEM] + [HBM] * 4,
        out_specs=[VMEM, VMEM, VMEM],
        out_shape=[jax.ShapeDtypeStruct((count, HEADS * HD), BF), kv_shape, kv_shape],
        scratch_shapes=[
            pltpu.VMEM((count, depth), BF),
            pltpu.VMEM((depth, HEADS * width), BF),
            pltpu.SemaphoreType.DMA((TOKEN_COPIES,)),
            pltpu.SemaphoreType.DMA((2,)),
        ],
        compiler_params=params(),
    )(pos, slope, seg_rows, seg_cols, *tokens, w_own, w_got)


def dense_kernel(pos, hidden, ctx, own, cross, *rest):
    halves, (out, normed, dense, sem) = rest[:4], rest[4:]
    y, m = pos[1], pos[2]
    size = own.shape[0]
    half = size // 2
    loads = [[pltpu.make_async_copy(own, dense.at[0], sem.at[0])], [pltpu.make_async_copy(cross, dense.at[1], sem.at[1])]]
    for r in (2, 3):
        copies = []
        for i in range(2):
            first = pl.multiple_of((y ^ i) * half, half)
            index = (r - 2) * 2 + i
            copies.append(pltpu.make_async_copy(halves[index], dense.at[r, pl.ds(first, half)], sem.at[2 + index]))
        loads.append(copies)
    for copies in loads:
        for copy in copies:
            copy.start()
    total = None
    for r in range(NM):
        owner = m ^ r
        left = jnp.concatenate([ctx[owner], ctx[NM + owner]], axis=1)
        for copy in loads[r]:
            copy.wait()
        term = jnp.dot(left, dense[r], preferred_element_type=F32).astype(BF).astype(F32)
        total = term if total is None else total + term
    stream = hidden[...].astype(F32) + total
    out[...] = stream.astype(BF)
    normed[...] = layer_norm(stream).astype(BF)


def dense_norm(pos, hidden, ctx, blocks):
    return pl.pallas_call(
        dense_kernel,
        in_specs=[SMEM, VMEM, VMEM] + [HBM] * len(blocks),
        out_specs=[VMEM, VMEM],
        out_shape=[jax.ShapeDtypeStruct(hidden.shape, BF)] * 2,
        scratch_shapes=[
            pltpu.VMEM((NM,) + blocks[0].shape, BF),
            pltpu.SemaphoreType.DMA((len(blocks),)),
        ],
        compiler_params=params(),
    )(pos, hidden, ctx, *blocks)


def up_kernel(count, half, pos, *refs):
    pieces, (near, *fars), (act, xbuf, wbuf, xsem, wsem) = refs[:count], refs[count:-5], refs[-5:]
    z = pos[0]
    rows, width = near.shape[1] // 2, wbuf.shape[3]
    loads = [[] for _ in range(NZ)]
    for side in range(2):
        src = near.at[:, side * rows : (side + 1) * rows]
        loads[side].append(pltpu.make_async_copy(src, wbuf.at[side], wsem.at[side, 0]))
        at = 0
        for i, far in enumerate(fars):
            part = far.shape[2]
            src = far.at[:, side * rows : (side + 1) * rows]
            r = 2 + (side ^ half)
            dst = wbuf.at[r, :, :, at : at + part]
            loads[r].append(pltpu.make_async_copy(src, dst, wsem.at[r, i]))
            at += part
    copies = []
    at = 0
    for i, piece in enumerate(pieces):
        copies.append(pltpu.make_async_copy(piece, xbuf.at[at : at + piece.shape[0]], xsem.at[i]))
        at += piece.shape[0]
    for copy in copies + [load for group in loads for load in group]:
        copy.start()
    for copy in copies:
        copy.wait()
    depth = wbuf.shape[1] * rows
    upper = None
    for r in range(NZ):
        for load in loads[r]:
            load.wait()
        left = xbuf[:, pl.ds(pl.multiple_of((z ^ r) * depth, depth), depth)]
        term = jnp.dot(left, wbuf[r].reshape(depth, width), preferred_element_type=F32)
        upper = term if upper is None else upper + term
    act[...] = jax.nn.gelu(upper, approximate=True).astype(BF)


def up_part(pos, half, pieces, near, fars):
    rows, depth = sum(piece.shape[0] for piece in pieces), pieces[0].shape[1]
    width = near.shape[2]
    return pl.pallas_call(
        functools.partial(up_kernel, len(pieces), half),
        in_specs=[SMEM] + [ANY] * len(pieces) + [HBM] * (1 + len(fars)),
        out_specs=VMEM,
        out_shape=jax.ShapeDtypeStruct((rows, width), BF),
        scratch_shapes=[
            pltpu.VMEM((rows, depth), BF),
            pltpu.VMEM((NZ, near.shape[0], near.shape[1] // 2, width), BF),
            pltpu.SemaphoreType.DMA((len(pieces),)),
            pltpu.SemaphoreType.DMA((NZ, len(fars))),
        ],
        compiler_params=params(),
    )(pos, *pieces, near, *fars)


def join_kernel(places, pos, *refs):
    *parts, out = refs
    z, y, m = pos[0], pos[1], pos[2]
    share = out.shape[0] // NM
    for part, (side, half, devices) in zip(parts, places):
        width = part.shape[1]
        columns = pl.ds(pl.multiple_of(((y ^ side) * 2 + (z % 2 ^ half)) * width, width), width)
        for i, r in enumerate(devices):
            rows = pl.ds(pl.multiple_of((m ^ r) * share, 16), share)
            out[rows, columns] = part[i * share : (i + 1) * share]


def join_parts(pos, shape, parts):
    return pl.pallas_call(
        functools.partial(join_kernel, [part[1:] for part in parts]),
        in_specs=[SMEM] + [VMEM] * len(parts),
        out_specs=VMEM,
        out_shape=jax.ShapeDtypeStruct(shape, BF),
        compiler_params=params(),
    )(pos, *(part[0] for part in parts))


def pages_kernel(pos, table, own, got, out):
    y = pos[1]
    for b in range(own.shape[0]):
        slot = table[0, b]
        for side, part in ((0, own), (1, got)):
            for h in range(HEADS):
                out[slot, :, (y ^ side) * HEADS + h] = part[b, :, h]


def place_pages(pos, table, own, got):
    blocks, two, heads, page, width = own.shape
    return pl.pallas_call(
        pages_kernel,
        in_specs=[SMEM, SMEM, VMEM, VMEM],
        out_specs=VMEM,
        out_shape=jax.ShapeDtypeStruct((blocks, two, NY * heads, page, width), BF),
        compiler_params=params(),
    )(pos, table, own, got)


def in_quad(copies):
    return lax.all_to_all(copies, AXES, split_axis=0, concat_axis=0, tiled=True, axis_index_groups=QUADS)


def local_planes(hidden_in, segment_ids, page_table, qkv_master, up_master, dense_weight):
    dp, mp = lax.axis_index("dp"), lax.axis_index("mp")
    z, y = dp // NY, dp % NY
    pos = jnp.stack([z, y, mp]).astype(jnp.int32)
    share = hidden_in.shape[0]
    head = H // NM * mp + HEADS * y + jnp.arange(HEADS)
    slopes = jnp.exp2(-8.0 * (head + 1).astype(F32) / H)

    qkv_own = to_all(cast_pieces(qkv_master))
    up_0, up_1 = cast_halves(pos, up_master)
    raw_0 = send(up_1, ZSWAP)
    normed = norm_rows(hidden_in)
    from_y = send(normed, YSWAP)
    from_x = send(normed, XSWAP)
    cross_low = send(from_y[: share // 2], XSWAP)
    cross_high = send(from_x[share // 2 :], YSWAP)
    mine = pack_rows(normed, from_y, from_x, cross_low, cross_high)
    half = dense_weight.shape[0] // 2
    give = lax.dynamic_slice_in_dim(dense_weight, y * half, half, 0)
    seg_other = send(segment_ids, YSWAP)
    segments = jnp.concatenate([segment_ids, seg_other], 0)
    seg_rows, seg_cols = segments[:, None, :], segments[:, :, None]
    qkv_own, mine, up_0, up_1, raw_0, give, seg_rows, seg_cols, slopes, pos, dense_own = window(
        qkv_own, mine, up_0, up_1, raw_0, give, seg_rows, seg_cols, slopes, pos, dense_weight
    )

    qkv_got = send(qkv_own, ZSWAP)
    near_w0 = in_plane(stack_rows(up_0, raw_0))
    other = send(mine, CORE)
    near = send(give, XSWAP)
    dense_c = send(dense_own, CORE)
    qkv_own, qkv_got, near_w0, up_0, up_1, mine, other, near, dense_own, dense_c = window(
        qkv_own, qkv_got, near_w0, up_0, up_1, mine, other, near, dense_own, dense_c
    )

    part = near_w0.shape[2] // 2
    far_a = send(near_w0[:, :, :part], ZFAR)
    raw_1 = send(up_0, ZSWAP)
    far = send(near, YSWAP)
    near_c = send(near, CORE)
    context, kv_own, kv_other = two_heads(pos, slopes, seg_rows, seg_cols, (mine, other), qkv_own, qkv_got)
    ctx_own = in_plane(context.reshape(PLANE, -1, HEADS * HD))
    near_w0, raw_1, up_1, far_a, ctx_own, near, far, near_c, dense_own, dense_c, kv_own, kv_other = window(
        near_w0, raw_1, up_1, far_a, ctx_own, near, far, near_c, dense_own, dense_c, kv_own, kv_other
    )

    far_b = send(near_w0[:, :, part:], ZFAR)
    near_w1 = in_plane(stack_rows(up_1, raw_1))
    got_a = send(far_a, ZSWAP)
    blocks = [dense_own, dense_c, near, far, near_c, send(far, CORE)]
    hidden_out, normed = dense_norm(pos, hidden_in, ctx_own, blocks)
    from_y = send(normed, YSWAP)
    from_x = send(normed, XSWAP)
    near_w0, near_w1, far_a, far_b, got_a, normed, from_y, from_x, kv_own, kv_other = window(
        near_w0, near_w1, far_a, far_b, got_a, normed, from_y, from_x, kv_own, kv_other
    )

    got_b = send(far_b, ZSWAP)
    cross_low = send(from_y[: share // 2], XSWAP)
    cross_high = send(from_x[share // 2 :], YSWAP)
    kv_got = send(window(kv_other, cross_high)[0], YSWAP)
    other = [from_y, cross_low, cross_high]
    other += [send(piece, CORE) for piece in other]
    own = [normed, from_x, send(normed, CORE), send(from_x, CORE)]
    near_w0, near_w1, far_a, far_b, got_a, *tokens = window(near_w0, near_w1, far_a, far_b, got_a, *other, *own)
    other, own = tokens[:6], tokens[6:]
    weights = [(near_w0, (far_a, far_b)), (near_w1, (got_a, got_b))]
    parts = []
    done = pos
    for half, side, pieces in ((0, 1, other), (1, 1, other), (0, 0, own), (1, 0, own)):
        first, _ = window(pieces[0], done)
        done = up_part(pos, half, [first] + pieces[1:], *weights[half])
        parts.append((send(done, YSWAP) if side else done, side, half, (0, 2, 1, 3)))
    activated = join_parts(pos, (NM * share, up_master.shape[1] // NM), parts)
    cache = place_pages(pos, page_table, kv_own, kv_got)
    return hidden_out, activated, cache


def solution(mesh):
    placed = (
        P(("dp", "mp"), None),
        P("dp", None),
        P("dp", None),
        P(("dp", "mp"), None),
        P(("dp", "mp"), None),
        P("mp", None),
    )
    planes = mesh.shape["dp"] == NZ * NY and mesh.shape["mp"] == NM
    return jax.shard_map(
        local_planes if planes else local_any,
        mesh=mesh,
        in_specs=placed,
        out_specs=(P(("dp", "mp"), None), P("dp", "mp"), P("dp", None, "mp", None, None)),
        check_vma=False,
    )
```

```python
import functools

import jax
import jax.numpy as jnp
from jax import lax
from jax.experimental import pallas as pl
from jax.experimental.pallas import tpu as pltpu
from jax.sharding import PartitionSpec as P

H = 16
HD = 128
PAGE = 128
AXES = ("dp", "mp")
BF = jnp.bfloat16
F32 = jnp.float32
VMEM_LIMIT = 56 * 1024 * 1024
SMALL_LIMIT = 16 * 1024 * 1024


def layer_norm(values):
    mean_val = jnp.mean(values, -1, keepdims=True)
    centered = values - mean_val
    variance = jnp.mean(centered * centered, -1, keepdims=True)
    return centered * lax.rsqrt(variance + 1e-05)


def attend(normed, qkv_w, segment, table, mp_index):
    group_rows = normed.shape[0]
    heads_dev = qkv_w.shape[1] // (3 * HD)
    joined = jnp.dot(normed, qkv_w, preferred_element_type=F32).astype(BF)
    joined = joined.reshape(group_rows, heads_dev, 3, HD)
    query = joined[:, :, 0]
    keys = joined[:, :, 1]
    vals = joined[:, :, 2]
    head_ids = mp_index * heads_dev + jnp.arange(heads_dev)
    slopes = jnp.exp2(-8.0 * (head_ids + 1).astype(F32) / H)
    positions = jnp.arange(group_rows)
    distance = (positions[:, None] - positions[None, :]).astype(F32)
    allowed = (segment[:, None] == segment[None, :]) & (distance >= 0)
    scores = jnp.einsum("thd,shd->hts", query, keys, preferred_element_type=F32) / jnp.sqrt(F32(HD))
    scores = scores - slopes[:, None, None] * distance[None]
    scores = jnp.where(allowed[None], scores, -jnp.inf)
    probs = jax.nn.softmax(scores, axis=-1).astype(BF)
    context = jnp.einsum("hts,shd->thd", probs, vals, preferred_element_type=F32).astype(BF)
    context = context.reshape(group_rows, heads_dev * HD)
    key_vals = jnp.stack([keys, vals], 1)
    pages_here = group_rows // PAGE
    key_vals = key_vals.reshape(pages_here, PAGE, 2, heads_dev, HD).transpose(0, 2, 3, 1, 4)
    cache = jnp.zeros((pages_here, 2, heads_dev, PAGE, HD), BF).at[table].set(key_vals)
    return context, cache


def local_any(hidden_in, segment_ids, page_table, qkv_master, up_master, dense_weight):
    mp_index = lax.axis_index("mp")

    def columns(master):
        mine = lax.all_to_all(master.astype(BF), "mp", split_axis=1, concat_axis=0, tiled=True)
        return lax.all_gather(mine, "dp", axis=0, tiled=True)

    qkv_w = columns(qkv_master)
    up_w = columns(up_master)
    normed_own = layer_norm(hidden_in.astype(F32)).astype(BF)
    normed = lax.all_gather(normed_own, "mp", axis=0, tiled=True)
    context, cache = attend(normed, qkv_w, segment_ids[0], page_table[0], mp_index)
    term = jnp.dot(context, dense_weight, preferred_element_type=F32).astype(BF)
    share = lax.psum_scatter(term, "mp", scatter_dimension=0, tiled=True).astype(F32)
    stream_own = hidden_in.astype(F32) + share
    normed_two = lax.all_gather(layer_norm(stream_own).astype(BF), "mp", axis=0, tiled=True)
    upper = jnp.dot(normed_two, up_w, preferred_element_type=F32)
    activated = jax.nn.gelu(upper, approximate=True).astype(BF)
    return stream_own.astype(BF), activated, cache


NZ, NY, NM = 4, 2, 4
PLANE = NY * NM
HEADS = H // PLANE


def pairs(move):
    out = []
    for z in range(NZ):
        for y in range(NY):
            for m in range(NM):
                to = move(z, y, m)
                if to is not None:
                    out.append(((z * NY + y) * NM + m, (to[0] * NY + to[1]) * NM + to[2]))
    return out


CORE = pairs(lambda z, y, m: (z, y, m ^ 1))
XSWAP = pairs(lambda z, y, m: (z, y, m ^ 2))
YSWAP = pairs(lambda z, y, m: (z, y ^ 1, m))
ZSWAP = pairs(lambda z, y, m: (z ^ 1, y, m))
ZFAR = pairs(lambda z, y, m: (z ^ 2, y, m))
PLANES = [[z * PLANE + i for i in range(PLANE)] for z in range(NZ)]
QUADS = [[z * PLANE + 2 * i + c for i in range(PLANE // 2)] for z in range(NZ) for c in range(2)]


def send(value, moves):
    return lax.ppermute(value, AXES, moves)


def window(*values):
    return lax.optimization_barrier(values)


def params(limit=VMEM_LIMIT):
    return pltpu.CompilerParams(vmem_limit_bytes=limit)


HBM = pl.BlockSpec(memory_space=pltpu.HBM)
ANY = pl.BlockSpec(memory_space=pl.ANY)
SMEM = pl.BlockSpec(memory_space=pltpu.SMEM)
VMEM = pl.BlockSpec(memory_space=pltpu.VMEM)


def cast_pieces(master):
    rows, cols = master.shape
    width = cols // PLANE // 2

    def kernel(src, dst):
        for p in range(PLANE):
            for part in range(2):
                start = ((2 * (p % NM) + p // NM) * 2 + part) * width
                piece = src[:, start : start + width].astype(BF)
                for z in range(part, NZ, 2):
                    dst[z * PLANE + p] = piece

    return pl.pallas_call(
        kernel,
        in_specs=[VMEM],
        out_specs=VMEM,
        out_shape=jax.ShapeDtypeStruct((NZ * PLANE, rows, width), BF),
        compiler_params=params(),
    )(master)


def cast_halves(pos, master):
    rows, cols = master.shape
    half = cols // PLANE // 2

    def kernel(pos, src, *dst):
        parity = pos[0] % 2
        for p in range(PLANE):
            start = (2 * (p % NM) + p // NM) * 2 * half
            for i in range(2):
                first = pl.multiple_of(start + (parity ^ i) * half, half)
                dst[i][p] = src[:, pl.ds(first, half)].astype(BF)

    shape = jax.ShapeDtypeStruct((PLANE, rows, half), BF)
    return pl.pallas_call(
        kernel,
        in_specs=[SMEM, VMEM],
        out_specs=[VMEM, VMEM],
        out_shape=[shape, shape],
        compiler_params=params(),
    )(pos, master)


def stack_kernel(own, got, out):
    rows = own.shape[1]
    out[:, :rows] = own[...]
    out[:, rows:] = got[...]


def stack_rows(own, got):
    count, rows, width = own.shape
    return pl.pallas_call(
        stack_kernel,
        in_specs=[VMEM, VMEM],
        out_specs=VMEM,
        out_shape=jax.ShapeDtypeStruct((count, 2 * rows, width), BF),
        compiler_params=params(),
    )(own, got)


def norm_kernel(hidden, out):
    out[...] = layer_norm(hidden[...].astype(F32)).astype(BF)


def norm_rows(hidden):
    return pl.pallas_call(
        norm_kernel,
        in_specs=[VMEM],
        out_specs=VMEM,
        out_shape=jax.ShapeDtypeStruct(hidden.shape, BF),
        compiler_params=params(),
    )(hidden)


def to_all(pieces):
    mine = lax.all_to_all(pieces, AXES, split_axis=0, concat_axis=0, tiled=True)
    return mine.reshape(-1, mine.shape[2])


def in_plane(pieces):
    return lax.all_to_all(pieces, AXES, split_axis=0, concat_axis=0, tiled=True, axis_index_groups=PLANES)


TOKEN_PIECES = 10


def token_copies(y, m, pieces, xbuf, sem):
    share = pieces[0].shape[0]
    half = share // 2
    place = [(0, 0, 0), (1, 0, 0), (0, 2, 0), (1, 2, 0), (1, 2, half)]
    place += [(dy, dm ^ 1, extra) for dy, dm, extra in place]
    copies = []
    for i, (dy, dm, extra) in enumerate(place):
        first = pl.multiple_of(((y ^ dy) * NM + (m ^ dm)) * share + extra, 16)
        copies.append(pltpu.make_async_copy(pieces[i], xbuf.at[pl.ds(first, pieces[i].shape[0])], sem.at[i]))
    return copies


def head_kernel(last, pos, slope, seg_rows, *refs):
    pieces, refs = refs[:TOKEN_PIECES], refs[TOKEN_PIECES:]
    if last:
        before, refs = refs[:3], refs[3:]
    weights, ctx, kv_own, kv_other, xbuf, wbuf, xsem, wsem = refs
    z, y, m = pos[0], pos[1], pos[2]
    copies = [pltpu.make_async_copy(weights, wbuf, wsem)] + token_copies(y, m, pieces, xbuf, xsem)
    for copy in copies:
        copy.start()
    group = xbuf.shape[0] // NY
    here = lax.broadcasted_iota(jnp.int32, (group, group), 0)
    there = lax.broadcasted_iota(jnp.int32, (group, group), 1)
    distance = here - there
    away = distance.astype(F32)
    h = 1 - z % 2 if last else z % 2
    if last:
        for src, dst in zip(before, (ctx, kv_own, kv_other)):
            dst[...] = src[...]
    for copy in copies:
        copy.wait()
    for g, kv in ((0, kv_own), (1, kv_other)):
        rows = pl.ds(pl.multiple_of((y ^ g) * group, group), group)
        seg_cols = jnp.broadcast_to(seg_rows[g], (PAGE, group)).T[:, :1]
        allowed = (seg_cols == seg_rows[g]) & (distance >= 0)
        joined = jnp.dot(xbuf[rows, :], wbuf[...], preferred_element_type=F32).astype(BF)
        query, keys, vals = (joined[:, j * HD : (j + 1) * HD] for j in range(3))
        scores = lax.dot_general(query, keys, (((1,), (1,)), ((), ())), preferred_element_type=F32)
        scores = scores * (1.0 / HD**0.5) - slope[h] * away
        scores = jnp.where(allowed, scores, -jnp.inf)
        raised = jnp.exp(scores - jnp.max(scores, -1, keepdims=True))
        probs = (raised * (1.0 / jnp.sum(raised, -1, keepdims=True))).astype(BF)
        result = jnp.dot(probs, vals, preferred_element_type=F32).astype(BF)
        ctx[rows, pl.ds(pl.multiple_of(h * HD, HD), HD)] = result
        for b in range(group // PAGE):
            kv[b, 0, h] = keys[b * PAGE : (b + 1) * PAGE]
            kv[b, 1, h] = vals[b * PAGE : (b + 1) * PAGE]


def one_head(pos, slope, seg_rows, tokens, weights, before=()):
    count, depth = PLANE * tokens[0].shape[0], tokens[0].shape[1]
    width = weights.shape[1]
    kv_shape = jax.ShapeDtypeStruct((count // NY // PAGE, 2, HEADS, PAGE, HD), BF)
    return pl.pallas_call(
        functools.partial(head_kernel, bool(before)),
        in_specs=[SMEM, SMEM, VMEM] + [ANY] * TOKEN_PIECES + [VMEM] * len(before) + [HBM],
        out_specs=[VMEM, VMEM, VMEM],
        out_shape=[jax.ShapeDtypeStruct((count, HEADS * HD), BF), kv_shape, kv_shape],
        scratch_shapes=[
            pltpu.VMEM((count, depth), BF),
            pltpu.VMEM((depth, width), BF),
            pltpu.SemaphoreType.DMA((TOKEN_PIECES,)),
            pltpu.SemaphoreType.DMA,
        ],
        compiler_params=params(),
    )(pos, slope, seg_rows, *tokens, *before, weights)


def dense_kernel(pos, hidden, ctx, own, cross, *rest):
    rows, (out, normed, dense, sem) = rest[:6], rest[6:]
    y, m = pos[1], pos[2]
    size = own.shape[0]
    half = size // 2
    loads = [[pltpu.make_async_copy(own, dense.at[0], sem.at[0])], [pltpu.make_async_copy(cross, dense.at[1], sem.at[1])]]
    for r in (2, 3):
        copies = []
        for i, first in enumerate((y * half, (1 - y) * half, (1 - y) * half + half // 2)):
            index = (r - 2) * 3 + i
            dst = dense.at[r, pl.ds(pl.multiple_of(first, half // 2), rows[index].shape[0])]
            copies.append(pltpu.make_async_copy(rows[index], dst, sem.at[2 + index]))
        loads.append(copies)
    for copies in loads:
        for copy in copies:
            copy.start()
    total = None
    for r in range(NM):
        owner = m ^ r
        left = jnp.concatenate([ctx[owner], ctx[NM + owner]], axis=1)
        for copy in loads[r]:
            copy.wait()
        term = jnp.dot(left, dense[r], preferred_element_type=F32).astype(BF).astype(F32)
        total = term if total is None else total + term
    stream = hidden[...].astype(F32) + total
    out[...] = stream.astype(BF)
    normed[...] = layer_norm(stream).astype(BF)


def dense_norm(pos, hidden, ctx, blocks):
    return pl.pallas_call(
        dense_kernel,
        in_specs=[SMEM, VMEM, VMEM] + [HBM] * len(blocks),
        out_specs=[VMEM, VMEM],
        out_shape=[jax.ShapeDtypeStruct(hidden.shape, BF)] * 2,
        scratch_shapes=[
            pltpu.VMEM((NM,) + blocks[0].shape, BF),
            pltpu.SemaphoreType.DMA((len(blocks),)),
        ],
        compiler_params=params(),
    )(pos, hidden, ctx, *blocks)


def up_kernel(count, half, pos, *refs):
    pieces, (*nears, far_a, far_b), (act, xbuf, wbuf, xsem, wsem) = refs[:count], refs[count:-5], refs[-5:]
    z = pos[0]
    fars = (far_a, far_b)
    rows, width = wbuf.shape[2], wbuf.shape[3]
    loads = [[] for _ in range(NZ)]
    for side in range(2):
        src = nears[side] if len(nears) == 2 else nears[0].at[:, side * rows : (side + 1) * rows]
        loads[side].append(pltpu.make_async_copy(src, wbuf.at[side], wsem.at[side, 0]))
        r = 2 + (side ^ half)
        at = 0
        for i, far in enumerate(fars):
            dst = wbuf.at[r, at : at + far.shape[0]]
            loads[r].append(pltpu.make_async_copy(far.at[:, side * rows : (side + 1) * rows], dst, wsem.at[r, i]))
            at += far.shape[0]
    copies = []
    at = 0
    for i, piece in enumerate(pieces):
        copies.append(pltpu.make_async_copy(piece, xbuf.at[at : at + piece.shape[0]], xsem.at[i]))
        at += piece.shape[0]
    for copy in copies + [load for group in loads for load in group]:
        copy.start()
    for copy in copies:
        copy.wait()
    depth = wbuf.shape[1] * rows
    upper = None
    for r in range(NZ):
        for load in loads[r]:
            load.wait()
        left = xbuf[:, pl.ds(pl.multiple_of((z ^ r) * depth, depth), depth)]
        term = jnp.dot(left, wbuf[r].reshape(depth, width), preferred_element_type=F32)
        upper = term if upper is None else upper + term
    act[...] = jax.nn.gelu(upper, approximate=True).astype(BF)


def up_part(pos, half, pieces, nears, fars):
    rows, depth = sum(piece.shape[0] for piece in pieces), pieces[0].shape[1]
    count, rows_in, width = 2 * fars[0].shape[0], fars[0].shape[1] // 2, nears[0].shape[2]
    return pl.pallas_call(
        functools.partial(up_kernel, len(pieces), half),
        in_specs=[SMEM] + [ANY] * len(pieces) + [HBM] * (len(nears) + len(fars)),
        out_specs=VMEM,
        out_shape=jax.ShapeDtypeStruct((rows, width), BF),
        scratch_shapes=[
            pltpu.VMEM((rows, depth), BF),
            pltpu.VMEM((NZ, count, rows_in, width), BF),
            pltpu.SemaphoreType.DMA((len(pieces),)),
            pltpu.SemaphoreType.DMA((NZ, len(fars))),
        ],
        compiler_params=params(SMALL_LIMIT),
    )(pos, *pieces, *nears, *fars)


def join_kernel(places, pos, *refs):
    *parts, out = refs
    z, y, m = pos[0], pos[1], pos[2]
    share = out.shape[0] // NM
    for part, (side, half, devices) in zip(parts, places):
        width = part.shape[1]
        columns = pl.ds(pl.multiple_of(((y ^ side) * 2 + (z % 2 ^ half)) * width, width), width)
        for i, r in enumerate(devices):
            rows = pl.ds(pl.multiple_of((m ^ r) * share, 16), share)
            out[rows, columns] = part[i * share : (i + 1) * share]


def join_parts(pos, shape, parts):
    return pl.pallas_call(
        functools.partial(join_kernel, [part[1:] for part in parts]),
        in_specs=[SMEM] + [VMEM] * len(parts),
        out_specs=VMEM,
        out_shape=jax.ShapeDtypeStruct(shape, BF),
        compiler_params=params(SMALL_LIMIT),
    )(pos, *(part[0] for part in parts))


def pages_kernel(pos, table, own, got, out):
    y = pos[1]
    for b in range(own.shape[0]):
        slot = table[0, b]
        for side, part in ((0, own), (1, got)):
            for h in range(HEADS):
                out[slot, :, (y ^ side) * HEADS + h] = part[b, :, h]


def place_pages(pos, table, own, got):
    blocks, two, heads, page, width = own.shape
    return pl.pallas_call(
        pages_kernel,
        in_specs=[SMEM, SMEM, VMEM, VMEM],
        out_specs=VMEM,
        out_shape=jax.ShapeDtypeStruct((blocks, two, NY * heads, page, width), BF),
        compiler_params=params(SMALL_LIMIT),
    )(pos, table, own, got)


def in_quad(copies):
    return lax.all_to_all(copies, AXES, split_axis=0, concat_axis=0, tiled=True, axis_index_groups=QUADS)


def local_planes(hidden_in, segment_ids, page_table, qkv_master, up_master, dense_weight):
    dp, mp = lax.axis_index("dp"), lax.axis_index("mp")
    z, y = dp // NY, dp % NY
    pos = jnp.stack([z, y, mp]).astype(jnp.int32)
    share = hidden_in.shape[0]
    head = H // NM * mp + HEADS * y + jnp.arange(HEADS)
    slopes = jnp.exp2(-8.0 * (head + 1).astype(F32) / H)

    qkv_own = to_all(cast_pieces(qkv_master))
    up_0, up_1 = cast_halves(pos, up_master)
    raw_0 = send(up_1, ZSWAP)
    normed = norm_rows(hidden_in)
    from_y = send(normed, YSWAP)
    from_x = send(normed, XSWAP)
    cross_low = send(from_y[: share // 2], XSWAP)
    cross_high = send(from_x[share // 2 :], YSWAP)
    tokens = [normed, from_y, from_x, cross_low, cross_high]
    half = dense_weight.shape[0] // 2
    give = lax.dynamic_slice_in_dim(dense_weight, y * half, half, 0)
    give_far = lax.dynamic_slice_in_dim(dense_weight, (1 - y) * half + half // 2, half // 2, 0)
    seg_other = send(segment_ids, YSWAP)
    segments = jnp.concatenate([segment_ids, seg_other], 0)
    seg_rows = segments[:, None, :]
    tokens += [send(piece, CORE) for piece in tokens[:3]]
    qkv_own, up_0, up_1, raw_0, give, give_far, seg_rows, slopes, pos, dense_own, *tokens = window(
        qkv_own, up_0, up_1, raw_0, give, give_far, seg_rows, slopes, pos, dense_weight, *tokens
    )

    qkv_got = send(qkv_own, ZSWAP)
    near_0 = in_plane(stack_rows(up_0, raw_0))
    near = send(give, XSWAP)
    dense_c = send(dense_own, CORE)
    tokens += [send(piece, CORE) for piece in tokens[3:5]]
    before = one_head(pos, slopes, seg_rows, tokens, qkv_own)
    qkv_got, near_0, up_1, near, give_far, dense_own, dense_c, *state = window(
        qkv_got, near_0, up_1, near, give_far, dense_own, dense_c, *tokens, *before
    )
    tokens, before = state[:TOKEN_PIECES], state[TOKEN_PIECES:]

    part = PLANE // 2
    far_a = send(near_0[:part], ZFAR)
    near_got = send(near_0[:, : near_0.shape[1] // 2], ZSWAP)
    far_y = send(near[: half // 2], YSWAP)
    far_x = send(give_far, XSWAP)
    context, kv_own, kv_other = one_head(pos, slopes, seg_rows, tokens, qkv_got, before)
    ctx_own = in_plane(context.reshape(PLANE, -1, HEADS * HD))
    kv_got = send(kv_other, YSWAP)
    near_0, near_got, up_1, far_a, ctx_own, near, far_y, far_x, dense_own, dense_c, kv_own, kv_got = window(
        near_0, near_got, up_1, far_a, ctx_own, near, far_y, far_x, dense_own, dense_c, kv_own, kv_got
    )

    far_b = send(near_0[part:], ZFAR)
    near_own = in_plane(up_1)
    got_a = send(far_a, ZSWAP)
    blocks = [dense_own, dense_c, near, far_y, far_x]
    blocks += [send(block, CORE) for block in blocks[2:]]
    hidden_out, normed = dense_norm(pos, hidden_in, ctx_own, blocks)
    from_y = send(normed, YSWAP)
    from_x = send(normed, XSWAP)
    near_0, near_own, near_got, far_a, far_b, got_a, normed, from_y, from_x, kv_own, kv_got = window(
        near_0, near_own, near_got, far_a, far_b, got_a, normed, from_y, from_x, kv_own, kv_got
    )

    got_b = send(far_b, ZSWAP)
    cross_low = send(from_y[: share // 2], XSWAP)
    cross_high = send(from_x[share // 2 :], YSWAP)
    other = [from_y, cross_low, cross_high]
    other += [send(piece, CORE) for piece in other]
    own = [normed, from_x, send(normed, CORE), send(from_x, CORE)]
    *tokens, near_0, far_a, far_b = window(*other, *own, near_0, far_a, far_b)
    other, own = tokens[:6], tokens[6:]
    weights = [((near_0,), (far_a, far_b)), ((near_own, near_got), (got_a, got_b))]
    parts = []
    done = pos
    for half, side, pieces in ((0, 1, other), (1, 1, other), (0, 0, own), (1, 0, own)):
        first, _ = window(pieces[0], done)
        done = up_part(pos, half, [first] + pieces[1:], *weights[half])
        parts.append((send(done, YSWAP) if side else done, side, half, (0, 2, 1, 3)))
    activated = join_parts(pos, (NM * share, up_master.shape[1] // NM), parts)
    cache = place_pages(pos, page_table, kv_own, kv_got)
    return hidden_out, activated, cache


def solution(mesh):
    placed = (
        P(("dp", "mp"), None),
        P("dp", None),
        P("dp", None),
        P(("dp", "mp"), None),
        P(("dp", "mp"), None),
        P("mp", None),
    )
    planes = mesh.shape["dp"] == NZ * NY and mesh.shape["mp"] == NM
    return jax.shard_map(
        local_planes if planes else local_any,
        mesh=mesh,
        in_specs=placed,
        out_specs=(P(("dp", "mp"), None), P("dp", "mp"), P("dp", None, "mp", None, None)),
        check_vma=False,
    )
```

```python
import functools

import jax
import jax.numpy as jnp
from jax import lax
from jax.experimental import pallas as pl
from jax.experimental.pallas import tpu as pltpu
from jax.sharding import PartitionSpec as P

H = 16
HD = 128
PAGE = 128
AXES = ("dp", "mp")
BF = jnp.bfloat16
F32 = jnp.float32
VMEM_LIMIT = 56 * 1024 * 1024
SMALL_LIMIT = 16 * 1024 * 1024


def layer_norm(values):
    mean_val = jnp.mean(values, -1, keepdims=True)
    centered = values - mean_val
    variance = jnp.mean(centered * centered, -1, keepdims=True)
    return centered * lax.rsqrt(variance + 1e-05)


def attend(normed, qkv_w, segment, table, mp_index):
    group_rows = normed.shape[0]
    heads_dev = qkv_w.shape[1] // (3 * HD)
    joined = jnp.dot(normed, qkv_w, preferred_element_type=F32).astype(BF)
    joined = joined.reshape(group_rows, heads_dev, 3, HD)
    query = joined[:, :, 0]
    keys = joined[:, :, 1]
    vals = joined[:, :, 2]
    head_ids = mp_index * heads_dev + jnp.arange(heads_dev)
    slopes = jnp.exp2(-8.0 * (head_ids + 1).astype(F32) / H)
    positions = jnp.arange(group_rows)
    distance = (positions[:, None] - positions[None, :]).astype(F32)
    allowed = (segment[:, None] == segment[None, :]) & (distance >= 0)
    scores = jnp.einsum("thd,shd->hts", query, keys, preferred_element_type=F32) / jnp.sqrt(F32(HD))
    scores = scores - slopes[:, None, None] * distance[None]
    scores = jnp.where(allowed[None], scores, -jnp.inf)
    probs = jax.nn.softmax(scores, axis=-1).astype(BF)
    context = jnp.einsum("hts,shd->thd", probs, vals, preferred_element_type=F32).astype(BF)
    context = context.reshape(group_rows, heads_dev * HD)
    key_vals = jnp.stack([keys, vals], 1)
    pages_here = group_rows // PAGE
    key_vals = key_vals.reshape(pages_here, PAGE, 2, heads_dev, HD).transpose(0, 2, 3, 1, 4)
    cache = jnp.zeros((pages_here, 2, heads_dev, PAGE, HD), BF).at[table].set(key_vals)
    return context, cache


def local_any(hidden_in, segment_ids, page_table, qkv_master, up_master, dense_weight):
    mp_index = lax.axis_index("mp")

    def columns(master):
        mine = lax.all_to_all(master.astype(BF), "mp", split_axis=1, concat_axis=0, tiled=True)
        return lax.all_gather(mine, "dp", axis=0, tiled=True)

    qkv_w = columns(qkv_master)
    up_w = columns(up_master)
    normed_own = layer_norm(hidden_in.astype(F32)).astype(BF)
    normed = lax.all_gather(normed_own, "mp", axis=0, tiled=True)
    context, cache = attend(normed, qkv_w, segment_ids[0], page_table[0], mp_index)
    term = jnp.dot(context, dense_weight, preferred_element_type=F32).astype(BF)
    share = lax.psum_scatter(term, "mp", scatter_dimension=0, tiled=True).astype(F32)
    stream_own = hidden_in.astype(F32) + share
    normed_two = lax.all_gather(layer_norm(stream_own).astype(BF), "mp", axis=0, tiled=True)
    upper = jnp.dot(normed_two, up_w, preferred_element_type=F32)
    activated = jax.nn.gelu(upper, approximate=True).astype(BF)
    return stream_own.astype(BF), activated, cache


NZ, NY, NM = 4, 2, 4
PLANE = NY * NM
HEADS = H // PLANE


def pairs(move):
    out = []
    for z in range(NZ):
        for y in range(NY):
            for m in range(NM):
                to = move(z, y, m)
                if to is not None:
                    out.append(((z * NY + y) * NM + m, (to[0] * NY + to[1]) * NM + to[2]))
    return out


CORE = pairs(lambda z, y, m: (z, y, m ^ 1))
XSWAP = pairs(lambda z, y, m: (z, y, m ^ 2))
YSWAP = pairs(lambda z, y, m: (z, y ^ 1, m))
ZSWAP = pairs(lambda z, y, m: (z ^ 1, y, m))
ZFAR = pairs(lambda z, y, m: (z ^ 2, y, m))
PLANES = [[z * PLANE + i for i in range(PLANE)] for z in range(NZ)]
QUADS = [[z * PLANE + 2 * i + c for i in range(PLANE // 2)] for z in range(NZ) for c in range(2)]


def send(value, moves):
    return lax.ppermute(value, AXES, moves)


def window(*values):
    return lax.optimization_barrier(values)


def params(limit=VMEM_LIMIT):
    return pltpu.CompilerParams(vmem_limit_bytes=limit)


HBM = pl.BlockSpec(memory_space=pltpu.HBM)
ANY = pl.BlockSpec(memory_space=pl.ANY)
SMEM = pl.BlockSpec(memory_space=pltpu.SMEM)
VMEM = pl.BlockSpec(memory_space=pltpu.VMEM)


def cast_pieces(master):
    rows, cols = master.shape
    width = cols // PLANE // 2

    def kernel(src, dst):
        for p in range(PLANE):
            for part in range(2):
                start = ((2 * (p % NM) + p // NM) * 2 + part) * width
                piece = src[:, start : start + width].astype(BF)
                for z in range(part, NZ, 2):
                    dst[z * PLANE + p] = piece

    return pl.pallas_call(
        kernel,
        in_specs=[VMEM],
        out_specs=VMEM,
        out_shape=jax.ShapeDtypeStruct((NZ * PLANE, rows, width), BF),
        compiler_params=params(),
    )(master)


def cast_and_norm(pos, master, hidden):
    rows, cols = master.shape
    half = cols // PLANE // 2

    def kernel(pos, src, hidden, first, second, normed):
        parity = pos[0] % 2
        for p in range(PLANE):
            start = (2 * (p % NM) + p // NM) * 2 * half
            for i, dst in ((0, first), (1, second)):
                column = pl.multiple_of(start + (parity ^ i) * half, half)
                dst[p] = src[:, pl.ds(column, half)].astype(BF)
        normed[...] = layer_norm(hidden[...].astype(F32)).astype(BF)

    shape = jax.ShapeDtypeStruct((PLANE, rows, half), BF)
    return pl.pallas_call(
        kernel,
        in_specs=[SMEM, VMEM, VMEM],
        out_specs=[VMEM, VMEM, VMEM],
        out_shape=[shape, shape, jax.ShapeDtypeStruct(hidden.shape, BF)],
        compiler_params=params(),
    )(pos, master, hidden)


def stack_kernel(own, got, out):
    rows = own.shape[1]
    out[:, :rows] = own[...]
    out[:, rows:] = got[...]


def stack_rows(own, got):
    count, rows, width = own.shape
    return pl.pallas_call(
        stack_kernel,
        in_specs=[VMEM, VMEM],
        out_specs=VMEM,
        out_shape=jax.ShapeDtypeStruct((count, 2 * rows, width), BF),
        compiler_params=params(),
    )(own, got)


def to_all(pieces):
    mine = lax.all_to_all(pieces, AXES, split_axis=0, concat_axis=0, tiled=True)
    return mine.reshape(-1, mine.shape[2])


def in_plane(pieces):
    return lax.all_to_all(pieces, AXES, split_axis=0, concat_axis=0, tiled=True, axis_index_groups=PLANES)


TOKEN_PIECES = 10


def token_copies(y, m, pieces, xbuf, sem):
    share = pieces[0].shape[0]
    half = share // 2
    place = [(0, 0, 0), (1, 0, 0), (0, 2, 0), (1, 2, 0), (1, 2, half)]
    place += [(dy, dm ^ 1, extra) for dy, dm, extra in place]
    copies = []
    for i, (dy, dm, extra) in enumerate(place):
        first = pl.multiple_of(((y ^ dy) * NM + (m ^ dm)) * share + extra, 16)
        copies.append(pltpu.make_async_copy(pieces[i], xbuf.at[pl.ds(first, pieces[i].shape[0])], sem.at[i]))
    return copies


def head_kernel(last, pos, slope, seg_rows, *refs):
    pieces, refs = refs[:TOKEN_PIECES], refs[TOKEN_PIECES:]
    if last:
        before, refs = refs[:3], refs[3:]
    weights, ctx, kv_own, kv_other, xbuf, wbuf, xsem, wsem = refs
    z, y, m = pos[0], pos[1], pos[2]
    copies = [pltpu.make_async_copy(weights, wbuf, wsem)] + token_copies(y, m, pieces, xbuf, xsem)
    for copy in copies:
        copy.start()
    group = xbuf.shape[0] // NY
    here = lax.broadcasted_iota(jnp.int32, (group, group), 0)
    there = lax.broadcasted_iota(jnp.int32, (group, group), 1)
    distance = here - there
    away = distance.astype(F32)
    h = 1 - z % 2 if last else z % 2
    if last:
        for src, dst in zip(before, (ctx, kv_own, kv_other)):
            dst[...] = src[...]
    for copy in copies:
        copy.wait()
    for g, kv in ((0, kv_own), (1, kv_other)):
        rows = pl.ds(pl.multiple_of((y ^ g) * group, group), group)
        seg_cols = jnp.broadcast_to(seg_rows[g], (PAGE, group)).T[:, :1]
        allowed = (seg_cols == seg_rows[g]) & (distance >= 0)
        joined = jnp.dot(xbuf[rows, :], wbuf[...], preferred_element_type=F32).astype(BF)
        query, keys, vals = (joined[:, j * HD : (j + 1) * HD] for j in range(3))
        scores = lax.dot_general(query, keys, (((1,), (1,)), ((), ())), preferred_element_type=F32)
        scores = scores * (1.0 / HD**0.5) - slope[h] * away
        scores = jnp.where(allowed, scores, -jnp.inf)
        raised = jnp.exp(scores - jnp.max(scores, -1, keepdims=True))
        probs = (raised * (1.0 / jnp.sum(raised, -1, keepdims=True))).astype(BF)
        result = jnp.dot(probs, vals, preferred_element_type=F32).astype(BF)
        ctx[rows, pl.ds(pl.multiple_of(h * HD, HD), HD)] = result
        for b in range(group // PAGE):
            kv[b, 0, h] = keys[b * PAGE : (b + 1) * PAGE]
            kv[b, 1, h] = vals[b * PAGE : (b + 1) * PAGE]


def one_head(pos, slope, seg_rows, tokens, weights, before=()):
    count, depth = PLANE * tokens[0].shape[0], tokens[0].shape[1]
    width = weights.shape[1]
    kv_shape = jax.ShapeDtypeStruct((count // NY // PAGE, 2, HEADS, PAGE, HD), BF)
    return pl.pallas_call(
        functools.partial(head_kernel, bool(before)),
        in_specs=[SMEM, SMEM, VMEM] + [ANY] * TOKEN_PIECES + [VMEM] * len(before) + [HBM],
        out_specs=[VMEM, VMEM, VMEM],
        out_shape=[jax.ShapeDtypeStruct((count, HEADS * HD), BF), kv_shape, kv_shape],
        scratch_shapes=[
            pltpu.VMEM((count, depth), BF),
            pltpu.VMEM((depth, width), BF),
            pltpu.SemaphoreType.DMA((TOKEN_PIECES,)),
            pltpu.SemaphoreType.DMA,
        ],
        compiler_params=params(),
    )(pos, slope, seg_rows, *tokens, *before, weights)


def dense_kernel(pos, hidden, ctx, own, cross, *rest):
    rows, (out, normed, dense, sem) = rest[:6], rest[6:]
    y, m = pos[1], pos[2]
    size = own.shape[0]
    half = size // 2
    loads = [[pltpu.make_async_copy(own, dense.at[0], sem.at[0])], [pltpu.make_async_copy(cross, dense.at[1], sem.at[1])]]
    for r in (2, 3):
        copies = []
        for i, first in enumerate((y * half, (1 - y) * half, (1 - y) * half + half // 2)):
            index = (r - 2) * 3 + i
            dst = dense.at[r, pl.ds(pl.multiple_of(first, half // 2), rows[index].shape[0])]
            copies.append(pltpu.make_async_copy(rows[index], dst, sem.at[2 + index]))
        loads.append(copies)
    for copies in loads:
        for copy in copies:
            copy.start()
    total = None
    for r in range(NM):
        owner = m ^ r
        left = jnp.concatenate([ctx[owner], ctx[NM + owner]], axis=1)
        for copy in loads[r]:
            copy.wait()
        term = jnp.dot(left, dense[r], preferred_element_type=F32).astype(BF).astype(F32)
        total = term if total is None else total + term
    stream = hidden[...].astype(F32) + total
    out[...] = stream.astype(BF)
    normed[...] = layer_norm(stream).astype(BF)


def dense_norm(pos, hidden, ctx, blocks):
    return pl.pallas_call(
        dense_kernel,
        in_specs=[SMEM, VMEM, VMEM] + [HBM] * 2 + [ANY] * (len(blocks) - 2),
        out_specs=[VMEM, VMEM],
        out_shape=[jax.ShapeDtypeStruct(hidden.shape, BF)] * 2,
        scratch_shapes=[
            pltpu.VMEM((NM,) + blocks[0].shape, BF),
            pltpu.SemaphoreType.DMA((len(blocks),)),
        ],
        compiler_params=params(),
    )(pos, hidden, ctx, *blocks)


def up_kernel(count, half, pos, *refs):
    pieces, (*nears, far_a, far_b), (act, xbuf, wbuf, xsem, wsem) = refs[:count], refs[count:-5], refs[-5:]
    z = pos[0]
    fars = (far_a, far_b)
    rows, width = wbuf.shape[2], wbuf.shape[3]
    loads = [[] for _ in range(NZ)]
    for side in range(2):
        src = nears[side] if len(nears) == 2 else nears[0].at[:, side * rows : (side + 1) * rows]
        loads[side].append(pltpu.make_async_copy(src, wbuf.at[side], wsem.at[side, 0]))
        r = 2 + (side ^ half)
        at = 0
        for i, far in enumerate(fars):
            dst = wbuf.at[r, at : at + far.shape[0]]
            loads[r].append(pltpu.make_async_copy(far.at[:, side * rows : (side + 1) * rows], dst, wsem.at[r, i]))
            at += far.shape[0]
    copies = []
    at = 0
    for i, piece in enumerate(pieces):
        copies.append(pltpu.make_async_copy(piece, xbuf.at[at : at + piece.shape[0]], xsem.at[i]))
        at += piece.shape[0]
    for copy in copies + [load for group in loads for load in group]:
        copy.start()
    for copy in copies:
        copy.wait()
    depth = wbuf.shape[1] * rows
    upper = None
    for r in range(NZ):
        for load in loads[r]:
            load.wait()
        left = xbuf[:, pl.ds(pl.multiple_of((z ^ r) * depth, depth), depth)]
        term = jnp.dot(left, wbuf[r].reshape(depth, width), preferred_element_type=F32)
        upper = term if upper is None else upper + term
    act[...] = jax.nn.gelu(upper, approximate=True).astype(BF)


def up_part(pos, half, pieces, nears, fars):
    rows, depth = sum(piece.shape[0] for piece in pieces), pieces[0].shape[1]
    count, rows_in, width = 2 * fars[0].shape[0], fars[0].shape[1] // 2, nears[0].shape[2]
    return pl.pallas_call(
        functools.partial(up_kernel, len(pieces), half),
        in_specs=[SMEM] + [ANY] * len(pieces) + [HBM] * (len(nears) + len(fars)),
        out_specs=VMEM,
        out_shape=jax.ShapeDtypeStruct((rows, width), BF),
        scratch_shapes=[
            pltpu.VMEM((rows, depth), BF),
            pltpu.VMEM((NZ, count, rows_in, width), BF),
            pltpu.SemaphoreType.DMA((len(pieces),)),
            pltpu.SemaphoreType.DMA((NZ, len(fars))),
        ],
        compiler_params=params(SMALL_LIMIT),
    )(pos, *pieces, *nears, *fars)


def join_copies(places, pos, parts, out, sem):
    z, y, m = pos[0], pos[1], pos[2]
    share = out.shape[0] // NM
    copies = []
    for part, (side, half, devices) in zip(parts, places):
        width = part.shape[1]
        columns = pl.ds(pl.multiple_of(((y ^ side) * 2 + (z % 2 ^ half)) * width, width), width)
        for i, r in enumerate(devices):
            rows = pl.ds(pl.multiple_of((m ^ r) * share, 16), share)
            src = part.at[i * share : (i + 1) * share]
            copies.append(pltpu.make_async_copy(src, out.at[rows, columns], sem.at[len(copies)]))
    return copies


def join_kernel(places, pos, *refs):
    *parts, out, sem = refs
    copies = join_copies(places, pos, parts[-len(places) :], out, sem)
    for copy in copies:
        copy.start()
    for copy in copies:
        copy.wait()


def join_parts(pos, shape, parts, before=None):
    places = [part[1:] for part in parts]
    started = [] if before is None else [before]
    return pl.pallas_call(
        functools.partial(join_kernel, places),
        in_specs=[SMEM] + [HBM] * len(started) + [ANY] * len(parts),
        out_specs=HBM,
        out_shape=jax.ShapeDtypeStruct(shape, BF),
        scratch_shapes=[pltpu.SemaphoreType.DMA((sum(len(devices) for _, _, devices in places),))],
        input_output_aliases={1: 0} if started else {},
        compiler_params=params(SMALL_LIMIT),
    )(pos, *started, *(part[0] for part in parts))


def pages_kernel(pos, table, own, got, out):
    y = pos[1]
    for b in range(own.shape[0]):
        slot = table[0, b]
        for side, part in ((0, own), (1, got)):
            for h in range(HEADS):
                out[slot, :, (y ^ side) * HEADS + h] = part[b, :, h]


def place_pages(pos, table, own, got):
    blocks, two, heads, page, width = own.shape
    return pl.pallas_call(
        pages_kernel,
        in_specs=[SMEM, SMEM, VMEM, VMEM],
        out_specs=VMEM,
        out_shape=jax.ShapeDtypeStruct((blocks, two, NY * heads, page, width), BF),
        compiler_params=params(SMALL_LIMIT),
    )(pos, table, own, got)


def in_quad(copies):
    return lax.all_to_all(copies, AXES, split_axis=0, concat_axis=0, tiled=True, axis_index_groups=QUADS)


def local_planes(hidden_in, segment_ids, page_table, qkv_master, up_master, dense_weight):
    dp, mp = lax.axis_index("dp"), lax.axis_index("mp")
    z, y = dp // NY, dp % NY
    pos = jnp.stack([z, y, mp]).astype(jnp.int32)
    share = hidden_in.shape[0]
    head = H // NM * mp + HEADS * y + jnp.arange(HEADS)
    slopes = jnp.exp2(-8.0 * (head + 1).astype(F32) / H)

    qkv_own = to_all(cast_pieces(qkv_master))
    up_0, up_1, normed = cast_and_norm(pos, up_master, hidden_in)
    raw_0 = send(up_1, ZSWAP)
    from_y = send(normed, YSWAP)
    from_x = send(normed, XSWAP)
    cross_low = send(from_y[: share // 2], XSWAP)
    cross_high = send(from_x[share // 2 :], YSWAP)
    tokens = [normed, from_y, from_x, cross_low, cross_high]
    half = dense_weight.shape[0] // 2
    give = lax.dynamic_slice_in_dim(dense_weight, y * half, half, 0)
    give_far = lax.dynamic_slice_in_dim(dense_weight, (1 - y) * half + half // 2, half // 2, 0)
    seg_other = send(segment_ids, YSWAP)
    segments = jnp.concatenate([segment_ids, seg_other], 0)
    seg_rows = segments[:, None, :]
    qkv_own, up_0, up_1, raw_0, give, give_far, seg_rows, slopes, pos, dense_own, *tokens = window(
        qkv_own, up_0, up_1, raw_0, give, give_far, seg_rows, slopes, pos, dense_weight, *tokens
    )

    qkv_got = send(qkv_own, ZSWAP)
    near_0 = in_plane(stack_rows(up_0, raw_0))
    near = send(give, XSWAP)
    dense_c = send(dense_own, CORE)
    tokens += [send(piece, CORE) for piece in tokens]
    before = one_head(pos, slopes, seg_rows, tokens, qkv_own)
    qkv_got, near_0, up_1, near, give_far, dense_own, dense_c, *state = window(
        qkv_got, near_0, up_1, near, give_far, dense_own, dense_c, *tokens, *before
    )
    tokens, before = state[:TOKEN_PIECES], state[TOKEN_PIECES:]

    part = PLANE // 2
    far_a = send(near_0[:part], ZFAR)
    near_got = send(near_0[:, : near_0.shape[1] // 2], ZSWAP)
    far_y = send(near[: half // 2], YSWAP)
    far_x = send(give_far, XSWAP)
    context, kv_own, kv_other = one_head(pos, slopes, seg_rows, tokens, qkv_got, before)
    ctx_own = in_plane(context.reshape(PLANE, -1, HEADS * HD))
    kv_got = send(kv_other, YSWAP)
    near_0, near_got, up_1, far_a, ctx_own, near, far_y, far_x, dense_own, dense_c, kv_own, kv_got = window(
        near_0, near_got, up_1, far_a, ctx_own, near, far_y, far_x, dense_own, dense_c, kv_own, kv_got
    )

    far_b = send(near_0[part:], ZFAR)
    near_own = in_plane(up_1)
    got_a = send(far_a, ZSWAP)
    blocks = [dense_own, dense_c, near, far_y, far_x]
    blocks += [send(block, CORE) for block in blocks[2:]]
    hidden_out, normed = dense_norm(pos, hidden_in, ctx_own, blocks)
    from_y = send(normed, YSWAP)
    from_x = send(normed, XSWAP)
    near_0, near_own, near_got, far_a, far_b, got_a, normed, from_y, from_x, kv_own, kv_got = window(
        near_0, near_own, near_got, far_a, far_b, got_a, normed, from_y, from_x, kv_own, kv_got
    )

    got_b = send(far_b, ZSWAP)
    cross_low = send(from_y[: share // 2], XSWAP)
    cross_high = send(from_x[share // 2 :], YSWAP)
    other = [from_y, cross_low, cross_high]
    other += [send(piece, CORE) for piece in other]
    own = [normed, from_x, send(normed, CORE), send(from_x, CORE)]
    *tokens, near_0, far_a, far_b = window(*other, *own, near_0, far_a, far_b)
    other, own = tokens[:6], tokens[6:]
    weights = [((near_0,), (far_a, far_b)), ((near_own, near_got), (got_a, got_b))]
    parts = []
    done = pos
    for half, side, pieces in ((0, 1, other), (1, 1, other), (0, 0, own), (1, 0, own)):
        first, _ = window(pieces[0], done)
        done = up_part(pos, half, [first] + pieces[1:], *weights[half])
        parts.append((send(done, YSWAP) if side else done, side, half, (0, 2, 1, 3)))
    shape = (NM * share, up_master.shape[1] // NM)
    activated = join_parts(pos, shape, [parts[0]] + parts[2:])
    activated = join_parts(pos, shape, parts[1:2], activated)
    cache = place_pages(pos, page_table, kv_own, kv_got)
    return hidden_out, activated, cache


def solution(mesh):
    placed = (
        P(("dp", "mp"), None),
        P("dp", None),
        P("dp", None),
        P(("dp", "mp"), None),
        P(("dp", "mp"), None),
        P("mp", None),
    )
    planes = mesh.shape["dp"] == NZ * NY and mesh.shape["mp"] == NM
    return jax.shard_map(
        local_planes if planes else local_any,
        mesh=mesh,
        in_specs=placed,
        out_specs=(P(("dp", "mp"), None), P("dp", "mp"), P("dp", None, "mp", None, None)),
        check_vma=False,
    )
```

```python
import functools

import jax
import jax.numpy as jnp
from jax import lax
from jax.experimental import pallas as pl
from jax.experimental.pallas import tpu as pltpu
from jax.sharding import PartitionSpec as P

H = 16
HD = 128
PAGE = 128
AXES = ("dp", "mp")
BF = jnp.bfloat16
F32 = jnp.float32
VMEM_LIMIT = 50 * 1024 * 1024
SMALL_LIMIT = 16 * 1024 * 1024


def layer_norm(values):
    mean_val = jnp.mean(values, -1, keepdims=True)
    centered = values - mean_val
    variance = jnp.mean(centered * centered, -1, keepdims=True)
    return centered * lax.rsqrt(variance + 1e-05)


def attend(normed, qkv_w, segment, table, mp_index):
    group_rows = normed.shape[0]
    heads_dev = qkv_w.shape[1] // (3 * HD)
    joined = jnp.dot(normed, qkv_w, preferred_element_type=F32).astype(BF)
    joined = joined.reshape(group_rows, heads_dev, 3, HD)
    query = joined[:, :, 0]
    keys = joined[:, :, 1]
    vals = joined[:, :, 2]
    head_ids = mp_index * heads_dev + jnp.arange(heads_dev)
    slopes = jnp.exp2(-8.0 * (head_ids + 1).astype(F32) / H)
    positions = jnp.arange(group_rows)
    distance = (positions[:, None] - positions[None, :]).astype(F32)
    allowed = (segment[:, None] == segment[None, :]) & (distance >= 0)
    scores = jnp.einsum("thd,shd->hts", query, keys, preferred_element_type=F32) / jnp.sqrt(F32(HD))
    scores = scores - slopes[:, None, None] * distance[None]
    scores = jnp.where(allowed[None], scores, -jnp.inf)
    probs = jax.nn.softmax(scores, axis=-1).astype(BF)
    context = jnp.einsum("hts,shd->thd", probs, vals, preferred_element_type=F32).astype(BF)
    context = context.reshape(group_rows, heads_dev * HD)
    key_vals = jnp.stack([keys, vals], 1)
    pages_here = group_rows // PAGE
    key_vals = key_vals.reshape(pages_here, PAGE, 2, heads_dev, HD).transpose(0, 2, 3, 1, 4)
    cache = jnp.zeros((pages_here, 2, heads_dev, PAGE, HD), BF).at[table].set(key_vals)
    return context, cache


def local_any(hidden_in, segment_ids, page_table, qkv_master, up_master, dense_weight):
    mp_index = lax.axis_index("mp")

    def columns(master):
        mine = lax.all_to_all(master.astype(BF), "mp", split_axis=1, concat_axis=0, tiled=True)
        return lax.all_gather(mine, "dp", axis=0, tiled=True)

    qkv_w = columns(qkv_master)
    up_w = columns(up_master)
    normed_own = layer_norm(hidden_in.astype(F32)).astype(BF)
    normed = lax.all_gather(normed_own, "mp", axis=0, tiled=True)
    context, cache = attend(normed, qkv_w, segment_ids[0], page_table[0], mp_index)
    term = jnp.dot(context, dense_weight, preferred_element_type=F32).astype(BF)
    share = lax.psum_scatter(term, "mp", scatter_dimension=0, tiled=True).astype(F32)
    stream_own = hidden_in.astype(F32) + share
    normed_two = lax.all_gather(layer_norm(stream_own).astype(BF), "mp", axis=0, tiled=True)
    upper = jnp.dot(normed_two, up_w, preferred_element_type=F32)
    activated = jax.nn.gelu(upper, approximate=True).astype(BF)
    return stream_own.astype(BF), activated, cache


NZ, NY, NM = 4, 2, 4
PLANE = NY * NM
HEADS = H // PLANE


def pairs(move):
    out = []
    for z in range(NZ):
        for y in range(NY):
            for m in range(NM):
                to = move(z, y, m)
                if to is not None:
                    out.append(((z * NY + y) * NM + m, (to[0] * NY + to[1]) * NM + to[2]))
    return out


CORE = pairs(lambda z, y, m: (z, y, m ^ 1))
XSWAP = pairs(lambda z, y, m: (z, y, m ^ 2))
YSWAP = pairs(lambda z, y, m: (z, y ^ 1, m))
ZSWAP = pairs(lambda z, y, m: (z ^ 1, y, m))
ZFAR = pairs(lambda z, y, m: (z ^ 2, y, m))
PLANES = [[z * PLANE + i for i in range(PLANE)] for z in range(NZ)]
QUADS = [[z * PLANE + 2 * i + c for i in range(PLANE // 2)] for z in range(NZ) for c in range(2)]


def send(value, moves):
    return lax.ppermute(value, AXES, moves)


def window(*values):
    return lax.optimization_barrier(values)


def params(limit=VMEM_LIMIT):
    return pltpu.CompilerParams(vmem_limit_bytes=limit)


HBM = pl.BlockSpec(memory_space=pltpu.HBM)
ANY = pl.BlockSpec(memory_space=pl.ANY)
SMEM = pl.BlockSpec(memory_space=pltpu.SMEM)
VMEM = pl.BlockSpec(memory_space=pltpu.VMEM)


def cast_pieces(master):
    rows, cols = master.shape
    width = cols // PLANE // 2

    def kernel(src, dst):
        for p in range(PLANE):
            for part in range(2):
                start = ((2 * (p % NM) + p // NM) * 2 + part) * width
                piece = src[:, start : start + width].astype(BF)
                for z in range(part, NZ, 2):
                    dst[z * PLANE + p] = piece

    return pl.pallas_call(
        kernel,
        in_specs=[VMEM],
        out_specs=VMEM,
        out_shape=jax.ShapeDtypeStruct((NZ * PLANE, rows, width), BF),
        compiler_params=params(),
    )(master)


def cast_and_norm(pos, master, hidden):
    rows, cols = master.shape
    half = cols // PLANE // 2

    def kernel(pos, src, hidden, first, second, normed):
        parity = pos[0] % 2
        for p in range(PLANE):
            start = (2 * (p % NM) + p // NM) * 2 * half
            for i, dst in ((0, first), (1, second)):
                column = pl.multiple_of(start + (parity ^ i) * half, half)
                dst[p] = src[:, pl.ds(column, half)].astype(BF)
        normed[...] = layer_norm(hidden[...].astype(F32)).astype(BF)

    shape = jax.ShapeDtypeStruct((PLANE, rows, half), BF)
    return pl.pallas_call(
        kernel,
        in_specs=[SMEM, VMEM, VMEM],
        out_specs=[VMEM, VMEM, VMEM],
        out_shape=[shape, shape, jax.ShapeDtypeStruct(hidden.shape, BF)],
        compiler_params=params(),
    )(pos, master, hidden)


def stack_kernel(own, got, out):
    rows = own.shape[1]
    out[:, :rows] = own[...]
    out[:, rows:] = got[...]


def stack_rows(own, got):
    count, rows, width = own.shape
    return pl.pallas_call(
        stack_kernel,
        in_specs=[VMEM, VMEM],
        out_specs=VMEM,
        out_shape=jax.ShapeDtypeStruct((count, 2 * rows, width), BF),
        compiler_params=params(),
    )(own, got)


def to_all(pieces):
    mine = lax.all_to_all(pieces, AXES, split_axis=0, concat_axis=0, tiled=True)
    return mine.reshape(-1, mine.shape[2])


def in_plane(pieces):
    return lax.all_to_all(pieces, AXES, split_axis=0, concat_axis=0, tiled=True, axis_index_groups=PLANES)


TOKEN_PIECES = 10


def token_copies(y, m, pieces, xbuf, sem):
    share = pieces[0].shape[0]
    half = share // 2
    place = [(0, 0, 0), (1, 0, 0), (0, 2, 0), (1, 2, 0), (1, 2, half)]
    place += [(dy, dm ^ 1, extra) for dy, dm, extra in place]
    copies = []
    for i, (dy, dm, extra) in enumerate(place):
        first = pl.multiple_of(((y ^ dy) * NM + (m ^ dm)) * share + extra, 16)
        copies.append(pltpu.make_async_copy(pieces[i], xbuf.at[pl.ds(first, pieces[i].shape[0])], sem.at[i]))
    return copies


def head_kernel(last, pos, slope, seg_rows, *refs):
    pieces, refs = refs[:TOKEN_PIECES], refs[TOKEN_PIECES:]
    if last:
        before, refs = refs[:3], refs[3:]
    weights, ctx, kv_own, kv_other, xbuf, wbuf, xsem, wsem = refs
    z, y, m = pos[0], pos[1], pos[2]
    copies = [pltpu.make_async_copy(weights, wbuf, wsem)] + token_copies(y, m, pieces, xbuf, xsem)
    for copy in copies:
        copy.start()
    group = xbuf.shape[0] // NY
    here = lax.broadcasted_iota(jnp.int32, (group, group), 0)
    there = lax.broadcasted_iota(jnp.int32, (group, group), 1)
    distance = here - there
    away = distance.astype(F32)
    h = 1 - z % 2 if last else z % 2
    if last:
        for src, dst in zip(before, (ctx, kv_own, kv_other)):
            dst[...] = src[...]
    for copy in copies:
        copy.wait()
    for g, kv in ((0, kv_own), (1, kv_other)):
        rows = pl.ds(pl.multiple_of((y ^ g) * group, group), group)
        seg_cols = jnp.broadcast_to(seg_rows[g], (PAGE, group)).T[:, :1]
        allowed = (seg_cols == seg_rows[g]) & (distance >= 0)
        joined = jnp.dot(xbuf[rows, :], wbuf[...], preferred_element_type=F32).astype(BF)
        query, keys, vals = (joined[:, j * HD : (j + 1) * HD] for j in range(3))
        scores = lax.dot_general(query, keys, (((1,), (1,)), ((), ())), preferred_element_type=F32)
        scores = scores * (1.0 / HD**0.5) - slope[h] * away
        scores = jnp.where(allowed, scores, -jnp.inf)
        raised = jnp.exp(scores - jnp.max(scores, -1, keepdims=True))
        probs = (raised * (1.0 / jnp.sum(raised, -1, keepdims=True))).astype(BF)
        result = jnp.dot(probs, vals, preferred_element_type=F32).astype(BF)
        ctx[rows, pl.ds(pl.multiple_of(h * HD, HD), HD)] = result
        for b in range(group // PAGE):
            kv[b, 0, h] = keys[b * PAGE : (b + 1) * PAGE]
            kv[b, 1, h] = vals[b * PAGE : (b + 1) * PAGE]


def one_head(pos, slope, seg_rows, tokens, weights, before=()):
    count, depth = PLANE * tokens[0].shape[0], tokens[0].shape[1]
    width = weights.shape[1]
    kv_shape = jax.ShapeDtypeStruct((count // NY // PAGE, 2, HEADS, PAGE, HD), BF)
    return pl.pallas_call(
        functools.partial(head_kernel, bool(before)),
        in_specs=[SMEM, SMEM, VMEM] + [ANY] * TOKEN_PIECES + [VMEM] * len(before) + [HBM],
        out_specs=[VMEM, VMEM, VMEM],
        out_shape=[jax.ShapeDtypeStruct((count, HEADS * HD), BF), kv_shape, kv_shape],
        scratch_shapes=[
            pltpu.VMEM((count, depth), BF),
            pltpu.VMEM((depth, width), BF),
            pltpu.SemaphoreType.DMA((TOKEN_PIECES,)),
            pltpu.SemaphoreType.DMA,
        ],
        compiler_params=params(),
    )(pos, slope, seg_rows, *tokens, *before, weights)


def dense_kernel(pos, hidden, ctx, own, cross, *rest):
    rows, (out, normed, dense, sem) = rest[:6], rest[6:]
    y, m = pos[1], pos[2]
    size = own.shape[0]
    half = size // 2
    loads = [[pltpu.make_async_copy(own, dense.at[0], sem.at[0])], [pltpu.make_async_copy(cross, dense.at[1], sem.at[1])]]
    for r in (2, 3):
        copies = []
        for i, first in enumerate((y * half, (1 - y) * half, (1 - y) * half + half // 2)):
            index = (r - 2) * 3 + i
            dst = dense.at[r, pl.ds(pl.multiple_of(first, half // 2), rows[index].shape[0])]
            copies.append(pltpu.make_async_copy(rows[index], dst, sem.at[2 + index]))
        loads.append(copies)
    for copies in loads:
        for copy in copies:
            copy.start()
    total = None
    for r in range(NM):
        owner = m ^ r
        left = jnp.concatenate([ctx[owner], ctx[NM + owner]], axis=1)
        for copy in loads[r]:
            copy.wait()
        term = jnp.dot(left, dense[r], preferred_element_type=F32).astype(BF).astype(F32)
        total = term if total is None else total + term
    stream = hidden[...].astype(F32) + total
    out[...] = stream.astype(BF)
    normed[...] = layer_norm(stream).astype(BF)


def dense_norm(pos, hidden, ctx, blocks):
    return pl.pallas_call(
        dense_kernel,
        in_specs=[SMEM, VMEM, VMEM] + [HBM] * 2 + [ANY] * (len(blocks) - 2),
        out_specs=[VMEM, VMEM],
        out_shape=[jax.ShapeDtypeStruct(hidden.shape, BF)] * 2,
        scratch_shapes=[
            pltpu.VMEM((NM,) + blocks[0].shape, BF),
            pltpu.SemaphoreType.DMA((len(blocks),)),
        ],
        compiler_params=params(),
    )(pos, hidden, ctx, *blocks)


def up_kernel(count, half, pos, *refs):
    pieces, (*nears, far_a, far_b), (act, xbuf, wbuf, xsem, wsem) = refs[:count], refs[count:-5], refs[-5:]
    z = pos[0]
    fars = (far_a, far_b)
    rows, width = wbuf.shape[2], wbuf.shape[3]
    loads = [[] for _ in range(NZ)]
    for side in range(2):
        src = nears[side] if len(nears) == 2 else nears[0].at[:, side * rows : (side + 1) * rows]
        loads[side].append(pltpu.make_async_copy(src, wbuf.at[side], wsem.at[side, 0]))
        r = 2 + (side ^ half)
        at = 0
        for i, far in enumerate(fars):
            dst = wbuf.at[r, at : at + far.shape[0]]
            loads[r].append(pltpu.make_async_copy(far.at[:, side * rows : (side + 1) * rows], dst, wsem.at[r, i]))
            at += far.shape[0]
    copies = []
    at = 0
    for i, piece in enumerate(pieces):
        copies.append(pltpu.make_async_copy(piece, xbuf.at[at : at + piece.shape[0]], xsem.at[i]))
        at += piece.shape[0]
    for copy in copies + [load for group in loads for load in group]:
        copy.start()
    for copy in copies:
        copy.wait()
    depth = wbuf.shape[1] * rows
    upper = None
    for r in range(NZ):
        for load in loads[r]:
            load.wait()
        left = xbuf[:, pl.ds(pl.multiple_of((z ^ r) * depth, depth), depth)]
        term = jnp.dot(left, wbuf[r].reshape(depth, width), preferred_element_type=F32)
        upper = term if upper is None else upper + term
    act[...] = jax.nn.gelu(upper, approximate=True).astype(BF)


def up_part(pos, half, pieces, nears, fars):
    rows, depth = sum(piece.shape[0] for piece in pieces), pieces[0].shape[1]
    count, rows_in, width = 2 * fars[0].shape[0], fars[0].shape[1] // 2, nears[0].shape[2]
    return pl.pallas_call(
        functools.partial(up_kernel, len(pieces), half),
        in_specs=[SMEM] + [ANY] * len(pieces) + [HBM] * (len(nears) + len(fars)),
        out_specs=VMEM,
        out_shape=jax.ShapeDtypeStruct((rows, width), BF),
        scratch_shapes=[
            pltpu.VMEM((rows, depth), BF),
            pltpu.VMEM((NZ, count, rows_in, width), BF),
            pltpu.SemaphoreType.DMA((len(pieces),)),
            pltpu.SemaphoreType.DMA((NZ, len(fars))),
        ],
        compiler_params=params(SMALL_LIMIT),
    )(pos, *pieces, *nears, *fars)


def join_copies(places, pos, parts, out, sem):
    z, y, m = pos[0], pos[1], pos[2]
    share = out.shape[0] // NM
    copies = []
    for part, (side, half, devices) in zip(parts, places):
        width = part.shape[1]
        columns = pl.ds(pl.multiple_of(((y ^ side) * 2 + (z % 2 ^ half)) * width, width), width)
        for i, r in enumerate(devices):
            rows = pl.ds(pl.multiple_of((m ^ r) * share, 16), share)
            src = part.at[i * share : (i + 1) * share]
            copies.append(pltpu.make_async_copy(src, out.at[rows, columns], sem.at[len(copies)]))
    return copies


def join_kernel(places, pos, *refs):
    *parts, out, sem = refs
    copies = join_copies(places, pos, parts[-len(places) :], out, sem)
    for copy in copies:
        copy.start()
    for copy in copies:
        copy.wait()


def join_parts(pos, shape, parts, before=None):
    places = [part[1:] for part in parts]
    started = [] if before is None else [before]
    return pl.pallas_call(
        functools.partial(join_kernel, places),
        in_specs=[SMEM] + [HBM] * len(started) + [ANY] * len(parts),
        out_specs=HBM,
        out_shape=jax.ShapeDtypeStruct(shape, BF),
        scratch_shapes=[pltpu.SemaphoreType.DMA((sum(len(devices) for _, _, devices in places),))],
        input_output_aliases={1: 0} if started else {},
        compiler_params=params(SMALL_LIMIT),
    )(pos, *started, *(part[0] for part in parts))


def pages_kernel(pos, table, own, got, out):
    y = pos[1]
    for b in range(own.shape[0]):
        slot = table[0, b]
        for side, part in ((0, own), (1, got)):
            for h in range(HEADS):
                out[slot, :, (y ^ side) * HEADS + h] = part[b, :, h]


def place_pages(pos, table, own, got):
    blocks, two, heads, page, width = own.shape
    return pl.pallas_call(
        pages_kernel,
        in_specs=[SMEM, SMEM, VMEM, VMEM],
        out_specs=VMEM,
        out_shape=jax.ShapeDtypeStruct((blocks, two, NY * heads, page, width), BF),
        compiler_params=params(SMALL_LIMIT),
    )(pos, table, own, got)


def in_quad(copies):
    return lax.all_to_all(copies, AXES, split_axis=0, concat_axis=0, tiled=True, axis_index_groups=QUADS)


def local_planes(hidden_in, segment_ids, page_table, qkv_master, up_master, dense_weight):
    dp, mp = lax.axis_index("dp"), lax.axis_index("mp")
    z, y = dp // NY, dp % NY
    pos = jnp.stack([z, y, mp]).astype(jnp.int32)
    share = hidden_in.shape[0]
    head = H // NM * mp + HEADS * y + jnp.arange(HEADS)
    slopes = jnp.exp2(-8.0 * (head + 1).astype(F32) / H)

    qkv_own = to_all(cast_pieces(qkv_master))
    up_0, up_1, normed = cast_and_norm(pos, up_master, hidden_in)
    raw_0 = send(up_1, ZSWAP)
    from_y = send(normed, YSWAP)
    from_x = send(normed, XSWAP)
    cross_low = send(from_y[: share // 2], XSWAP)
    cross_high = send(from_x[share // 2 :], YSWAP)
    tokens = [normed, from_y, from_x, cross_low, cross_high]
    half = dense_weight.shape[0] // 2
    give = lax.dynamic_slice_in_dim(dense_weight, y * half, half, 0)
    give_far = lax.dynamic_slice_in_dim(dense_weight, (1 - y) * half + half // 2, half // 2, 0)
    seg_other = send(segment_ids, YSWAP)
    segments = jnp.concatenate([segment_ids, seg_other], 0)
    seg_rows = segments[:, None, :]
    qkv_own, up_0, up_1, raw_0, give, give_far, seg_rows, slopes, pos, dense_own, *tokens = window(
        qkv_own, up_0, up_1, raw_0, give, give_far, seg_rows, slopes, pos, dense_weight, *tokens
    )

    qkv_got = send(qkv_own, ZSWAP)
    near_0 = in_plane(stack_rows(up_0, raw_0))
    near = send(give, XSWAP)
    dense_c = send(dense_own, CORE)
    tokens += [send(piece, CORE) for piece in tokens]
    before = one_head(pos, slopes, seg_rows, tokens, qkv_own)
    qkv_got, near_0, up_1, near, give_far, dense_own, dense_c, *state = window(
        qkv_got, near_0, up_1, near, give_far, dense_own, dense_c, *tokens, *before
    )
    tokens, before = state[:TOKEN_PIECES], state[TOKEN_PIECES:]

    part = PLANE // 2
    far_a = send(near_0[:part], ZFAR)
    near_got = send(near_0[:, : near_0.shape[1] // 2], ZSWAP)
    far_y = send(near[: half // 2], YSWAP)
    far_x = send(give_far, XSWAP)
    context, kv_own, kv_other = one_head(pos, slopes, seg_rows, tokens, qkv_got, before)
    ctx_own = in_plane(context.reshape(PLANE, -1, HEADS * HD))
    kv_got = send(kv_other, YSWAP)
    near_0, near_got, up_1, far_a, ctx_own, near, far_y, far_x, dense_own, dense_c, kv_own, kv_got = window(
        near_0, near_got, up_1, far_a, ctx_own, near, far_y, far_x, dense_own, dense_c, kv_own, kv_got
    )

    far_b = send(near_0[part:], ZFAR)
    near_own = in_plane(up_1)
    got_a = send(far_a, ZSWAP)
    blocks = [dense_own, dense_c, near, far_y, far_x]
    blocks += [send(block, CORE) for block in blocks[2:]]
    hidden_out, normed = dense_norm(pos, hidden_in, ctx_own, blocks)
    from_y = send(normed, YSWAP)
    from_x = send(normed, XSWAP)
    near_0, near_own, near_got, far_a, far_b, got_a, normed, from_y, from_x, kv_own, kv_got = window(
        near_0, near_own, near_got, far_a, far_b, got_a, normed, from_y, from_x, kv_own, kv_got
    )

    got_b = send(far_b, ZSWAP)
    cross_low = send(from_y[: share // 2], XSWAP)
    cross_high = send(from_x[share // 2 :], YSWAP)
    other = [from_y, cross_low, cross_high]
    other += [send(piece, CORE) for piece in other]
    own = [normed, from_x, send(normed, CORE), send(from_x, CORE)]
    *tokens, near_0, far_a, far_b = window(*other, *own, near_0, far_a, far_b)
    other, own = tokens[:6], tokens[6:]
    weights = [((near_0,), (far_a, far_b)), ((near_own, near_got), (got_a, got_b))]
    parts = []
    done = pos
    for half, side, pieces in ((0, 1, other), (1, 1, other), (0, 0, own), (1, 0, own)):
        first, _ = window(pieces[0], done)
        done = up_part(pos, half, [first] + pieces[1:], *weights[half])
        parts.append((send(done, YSWAP) if side else done, side, half, (0, 2, 1, 3)))
    shape = (NM * share, up_master.shape[1] // NM)
    activated = join_parts(pos, shape, [parts[0]] + parts[2:])
    activated = join_parts(pos, shape, parts[1:2], activated)
    cache = place_pages(pos, page_table, kv_own, kv_got)
    return hidden_out, activated, cache


def solution(mesh):
    placed = (
        P(("dp", "mp"), None),
        P("dp", None),
        P("dp", None),
        P(("dp", "mp"), None),
        P(("dp", "mp"), None),
        P("mp", None),
    )
    planes = mesh.shape["dp"] == NZ * NY and mesh.shape["mp"] == NM
    return jax.shard_map(
        local_planes if planes else local_any,
        mesh=mesh,
        in_specs=placed,
        out_specs=(P(("dp", "mp"), None), P("dp", "mp"), P("dp", None, "mp", None, None)),
        check_vma=False,
    )
```

```python
import functools

import jax
import jax.numpy as jnp
from jax import lax
from jax.experimental import pallas as pl
from jax.experimental.pallas import tpu as pltpu
from jax.sharding import PartitionSpec as P

H = 16
HD = 128
PAGE = 128
AXES = ("dp", "mp")
BF = jnp.bfloat16
F32 = jnp.float32
VMEM_LIMIT = 50 * 1024 * 1024
SMALL_LIMIT = 16 * 1024 * 1024


def layer_norm(values):
    mean_val = jnp.mean(values, -1, keepdims=True)
    centered = values - mean_val
    variance = jnp.mean(centered * centered, -1, keepdims=True)
    return centered * lax.rsqrt(variance + 1e-05)


def attend(normed, qkv_w, segment, table, mp_index):
    group_rows = normed.shape[0]
    heads_dev = qkv_w.shape[1] // (3 * HD)
    joined = jnp.dot(normed, qkv_w, preferred_element_type=F32).astype(BF)
    joined = joined.reshape(group_rows, heads_dev, 3, HD)
    query = joined[:, :, 0]
    keys = joined[:, :, 1]
    vals = joined[:, :, 2]
    head_ids = mp_index * heads_dev + jnp.arange(heads_dev)
    slopes = jnp.exp2(-8.0 * (head_ids + 1).astype(F32) / H)
    positions = jnp.arange(group_rows)
    distance = (positions[:, None] - positions[None, :]).astype(F32)
    allowed = (segment[:, None] == segment[None, :]) & (distance >= 0)
    scores = jnp.einsum("thd,shd->hts", query, keys, preferred_element_type=F32) / jnp.sqrt(F32(HD))
    scores = scores - slopes[:, None, None] * distance[None]
    scores = jnp.where(allowed[None], scores, -jnp.inf)
    probs = jax.nn.softmax(scores, axis=-1).astype(BF)
    context = jnp.einsum("hts,shd->thd", probs, vals, preferred_element_type=F32).astype(BF)
    context = context.reshape(group_rows, heads_dev * HD)
    key_vals = jnp.stack([keys, vals], 1)
    pages_here = group_rows // PAGE
    key_vals = key_vals.reshape(pages_here, PAGE, 2, heads_dev, HD).transpose(0, 2, 3, 1, 4)
    cache = jnp.zeros((pages_here, 2, heads_dev, PAGE, HD), BF).at[table].set(key_vals)
    return context, cache


def local_any(hidden_in, segment_ids, page_table, qkv_master, up_master, dense_weight):
    mp_index = lax.axis_index("mp")

    def columns(master):
        mine = lax.all_to_all(master.astype(BF), "mp", split_axis=1, concat_axis=0, tiled=True)
        return lax.all_gather(mine, "dp", axis=0, tiled=True)

    qkv_w = columns(qkv_master)
    up_w = columns(up_master)
    normed_own = layer_norm(hidden_in.astype(F32)).astype(BF)
    normed = lax.all_gather(normed_own, "mp", axis=0, tiled=True)
    context, cache = attend(normed, qkv_w, segment_ids[0], page_table[0], mp_index)
    term = jnp.dot(context, dense_weight, preferred_element_type=F32).astype(BF)
    share = lax.psum_scatter(term, "mp", scatter_dimension=0, tiled=True).astype(F32)
    stream_own = hidden_in.astype(F32) + share
    normed_two = lax.all_gather(layer_norm(stream_own).astype(BF), "mp", axis=0, tiled=True)
    upper = jnp.dot(normed_two, up_w, preferred_element_type=F32)
    activated = jax.nn.gelu(upper, approximate=True).astype(BF)
    return stream_own.astype(BF), activated, cache


NZ, NY, NM = 4, 2, 4
PLANE = NY * NM
HEADS = H // PLANE


def pairs(move):
    out = []
    for z in range(NZ):
        for y in range(NY):
            for m in range(NM):
                to = move(z, y, m)
                if to is not None:
                    out.append(((z * NY + y) * NM + m, (to[0] * NY + to[1]) * NM + to[2]))
    return out


CORE = pairs(lambda z, y, m: (z, y, m ^ 1))
XSWAP = pairs(lambda z, y, m: (z, y, m ^ 2))
YSWAP = pairs(lambda z, y, m: (z, y ^ 1, m))
ZSWAP = pairs(lambda z, y, m: (z ^ 1, y, m))
ZFAR = pairs(lambda z, y, m: (z ^ 2, y, m))
PLANES = [[z * PLANE + i for i in range(PLANE)] for z in range(NZ)]
QUADS = [[z * PLANE + 2 * i + c for i in range(PLANE // 2)] for z in range(NZ) for c in range(2)]


def send(value, moves):
    return lax.ppermute(value, AXES, moves)


def window(*values):
    return lax.optimization_barrier(values)


def params(limit=VMEM_LIMIT):
    return pltpu.CompilerParams(vmem_limit_bytes=limit)


HBM = pl.BlockSpec(memory_space=pltpu.HBM)
ANY = pl.BlockSpec(memory_space=pl.ANY)
SMEM = pl.BlockSpec(memory_space=pltpu.SMEM)
VMEM = pl.BlockSpec(memory_space=pltpu.VMEM)


def cast_pieces(master):
    rows, cols = master.shape
    width = cols // PLANE // 2

    def kernel(src, dst):
        for p in range(PLANE):
            for part in range(2):
                start = ((2 * (p % NM) + p // NM) * 2 + part) * width
                piece = src[:, start : start + width].astype(BF)
                for z in range(part, NZ, 2):
                    dst[z * PLANE + p] = piece

    return pl.pallas_call(
        kernel,
        in_specs=[VMEM],
        out_specs=VMEM,
        out_shape=jax.ShapeDtypeStruct((NZ * PLANE, rows, width), BF),
        compiler_params=params(),
    )(master)


def cast_and_norm(pos, master, hidden):
    rows, cols = master.shape
    half = cols // PLANE // 2

    def kernel(pos, src, hidden, first, second, normed):
        parity = pos[0] % 2
        for p in range(PLANE):
            start = (2 * (p % NM) + p // NM) * 2 * half
            for i, dst in ((0, first), (1, second)):
                column = pl.multiple_of(start + (parity ^ i) * half, half)
                dst[p] = src[:, pl.ds(column, half)].astype(BF)
        normed[...] = layer_norm(hidden[...].astype(F32)).astype(BF)

    shape = jax.ShapeDtypeStruct((PLANE, rows, half), BF)
    return pl.pallas_call(
        kernel,
        in_specs=[SMEM, VMEM, VMEM],
        out_specs=[VMEM, VMEM, VMEM],
        out_shape=[shape, shape, jax.ShapeDtypeStruct(hidden.shape, BF)],
        compiler_params=params(),
    )(pos, master, hidden)


def stack_kernel(own, got, out):
    rows = own.shape[1]
    out[:, :rows] = own[...]
    out[:, rows:] = got[...]


def stack_rows(own, got):
    count, rows, width = own.shape
    step = count // 4
    return pl.pallas_call(
        stack_kernel,
        grid=(count // step,),
        in_specs=[pl.BlockSpec((step, rows, width), lambda i: (i, 0, 0))] * 2,
        out_specs=pl.BlockSpec((step, 2 * rows, width), lambda i: (i, 0, 0)),
        out_shape=jax.ShapeDtypeStruct((count, 2 * rows, width), BF),
        compiler_params=params(),
    )(own, got)


def to_all(pieces):
    mine = lax.all_to_all(pieces, AXES, split_axis=0, concat_axis=0, tiled=True)
    return mine.reshape(-1, mine.shape[2])


def in_plane(pieces):
    return lax.all_to_all(pieces, AXES, split_axis=0, concat_axis=0, tiled=True, axis_index_groups=PLANES)


TOKEN_PIECES = 10


def token_copies(y, m, pieces, xbuf, sem):
    share = pieces[0].shape[0]
    half = share // 2
    place = [(0, 0, 0), (1, 0, 0), (0, 2, 0), (1, 2, 0), (1, 2, half)]
    place += [(dy, dm ^ 1, extra) for dy, dm, extra in place]
    copies = []
    for i, (dy, dm, extra) in enumerate(place):
        first = pl.multiple_of(((y ^ dy) * NM + (m ^ dm)) * share + extra, 16)
        copies.append(pltpu.make_async_copy(pieces[i], xbuf.at[pl.ds(first, pieces[i].shape[0])], sem.at[i]))
    return copies


def head_kernel(last, pos, slope, seg_rows, *refs):
    pieces, refs = refs[:TOKEN_PIECES], refs[TOKEN_PIECES:]
    if last:
        before, refs = refs[:3], refs[3:]
    weights, ctx, kv_own, kv_other, xbuf, wbuf, xsem, wsem = refs
    z, y, m = pos[0], pos[1], pos[2]
    copies = [pltpu.make_async_copy(weights, wbuf, wsem)] + token_copies(y, m, pieces, xbuf, xsem)
    for copy in copies:
        copy.start()
    group = xbuf.shape[0] // NY
    here = lax.broadcasted_iota(jnp.int32, (group, group), 0)
    there = lax.broadcasted_iota(jnp.int32, (group, group), 1)
    distance = here - there
    away = distance.astype(F32)
    h = 1 - z % 2 if last else z % 2
    if last:
        for src, dst in zip(before, (ctx, kv_own, kv_other)):
            dst[...] = src[...]
    for copy in copies:
        copy.wait()
    for g, kv in ((0, kv_own), (1, kv_other)):
        rows = pl.ds(pl.multiple_of((y ^ g) * group, group), group)
        seg_cols = jnp.broadcast_to(seg_rows[g], (PAGE, group)).T[:, :1]
        allowed = (seg_cols == seg_rows[g]) & (distance >= 0)
        joined = jnp.dot(xbuf[rows, :], wbuf[...], preferred_element_type=F32).astype(BF)
        query, keys, vals = (joined[:, j * HD : (j + 1) * HD] for j in range(3))
        scores = lax.dot_general(query, keys, (((1,), (1,)), ((), ())), preferred_element_type=F32)
        scores = scores * (1.0 / HD**0.5) - slope[h] * away
        scores = jnp.where(allowed, scores, -jnp.inf)
        raised = jnp.exp(scores - jnp.max(scores, -1, keepdims=True))
        probs = (raised * (1.0 / jnp.sum(raised, -1, keepdims=True))).astype(BF)
        result = jnp.dot(probs, vals, preferred_element_type=F32).astype(BF)
        ctx[rows, pl.ds(pl.multiple_of(h * HD, HD), HD)] = result
        for b in range(group // PAGE):
            kv[b, 0, h] = keys[b * PAGE : (b + 1) * PAGE]
            kv[b, 1, h] = vals[b * PAGE : (b + 1) * PAGE]


def one_head(pos, slope, seg_rows, tokens, weights, before=()):
    count, depth = PLANE * tokens[0].shape[0], tokens[0].shape[1]
    width = weights.shape[1]
    kv_shape = jax.ShapeDtypeStruct((count // NY // PAGE, 2, HEADS, PAGE, HD), BF)
    return pl.pallas_call(
        functools.partial(head_kernel, bool(before)),
        in_specs=[SMEM, SMEM, VMEM] + [ANY] * TOKEN_PIECES + [VMEM] * len(before) + [HBM],
        out_specs=[VMEM, VMEM, VMEM],
        out_shape=[jax.ShapeDtypeStruct((count, HEADS * HD), BF), kv_shape, kv_shape],
        scratch_shapes=[
            pltpu.VMEM((count, depth), BF),
            pltpu.VMEM((depth, width), BF),
            pltpu.SemaphoreType.DMA((TOKEN_PIECES,)),
            pltpu.SemaphoreType.DMA,
        ],
        compiler_params=params(),
    )(pos, slope, seg_rows, *tokens, *before, weights)


def dense_kernel(pos, hidden, ctx, own, cross, *rest):
    rows, (out, normed, dense, sem) = rest[:6], rest[6:]
    y, m = pos[1], pos[2]
    size = own.shape[0]
    half = size // 2
    loads = [[pltpu.make_async_copy(own, dense.at[0], sem.at[0])], [pltpu.make_async_copy(cross, dense.at[1], sem.at[1])]]
    for r in (2, 3):
        copies = []
        for i, first in enumerate((y * half, (1 - y) * half, (1 - y) * half + half // 2)):
            index = (r - 2) * 3 + i
            dst = dense.at[r, pl.ds(pl.multiple_of(first, half // 2), rows[index].shape[0])]
            copies.append(pltpu.make_async_copy(rows[index], dst, sem.at[2 + index]))
        loads.append(copies)
    for copies in loads:
        for copy in copies:
            copy.start()
    total = None
    for r in range(NM):
        owner = m ^ r
        left = jnp.concatenate([ctx[owner], ctx[NM + owner]], axis=1)
        for copy in loads[r]:
            copy.wait()
        term = jnp.dot(left, dense[r], preferred_element_type=F32).astype(BF).astype(F32)
        total = term if total is None else total + term
    stream = hidden[...].astype(F32) + total
    out[...] = stream.astype(BF)
    normed[...] = layer_norm(stream).astype(BF)


def dense_norm(pos, hidden, ctx, blocks):
    return pl.pallas_call(
        dense_kernel,
        in_specs=[SMEM, VMEM, VMEM] + [HBM] * 2 + [ANY] * (len(blocks) - 2),
        out_specs=[VMEM, VMEM],
        out_shape=[jax.ShapeDtypeStruct(hidden.shape, BF)] * 2,
        scratch_shapes=[
            pltpu.VMEM((NM,) + blocks[0].shape, BF),
            pltpu.SemaphoreType.DMA((len(blocks),)),
        ],
        compiler_params=params(),
    )(pos, hidden, ctx, *blocks)


def up_kernel(count, half, pos, *refs):
    pieces, (*nears, far_a, far_b), (act, xbuf, wbuf, xsem, wsem) = refs[:count], refs[count:-5], refs[-5:]
    z = pos[0]
    fars = (far_a, far_b)
    rows, width = wbuf.shape[2], wbuf.shape[3]
    loads = [[] for _ in range(NZ)]
    for side in range(2):
        src = nears[side] if len(nears) == 2 else nears[0].at[:, side * rows : (side + 1) * rows]
        loads[side].append(pltpu.make_async_copy(src, wbuf.at[side], wsem.at[side, 0]))
        r = 2 + (side ^ half)
        at = 0
        for i, far in enumerate(fars):
            dst = wbuf.at[r, at : at + far.shape[0]]
            loads[r].append(pltpu.make_async_copy(far.at[:, side * rows : (side + 1) * rows], dst, wsem.at[r, i]))
            at += far.shape[0]
    copies = []
    at = 0
    for i, piece in enumerate(pieces):
        copies.append(pltpu.make_async_copy(piece, xbuf.at[at : at + piece.shape[0]], xsem.at[i]))
        at += piece.shape[0]
    for copy in copies + [load for group in loads for load in group]:
        copy.start()
    for copy in copies:
        copy.wait()
    depth = wbuf.shape[1] * rows
    upper = None
    for r in range(NZ):
        for load in loads[r]:
            load.wait()
        left = xbuf[:, pl.ds(pl.multiple_of((z ^ r) * depth, depth), depth)]
        term = jnp.dot(left, wbuf[r].reshape(depth, width), preferred_element_type=F32)
        upper = term if upper is None else upper + term
    act[...] = jax.nn.gelu(upper, approximate=True).astype(BF)


def up_part(pos, half, pieces, nears, fars):
    rows, depth = sum(piece.shape[0] for piece in pieces), pieces[0].shape[1]
    count, rows_in, width = 2 * fars[0].shape[0], fars[0].shape[1] // 2, nears[0].shape[2]
    return pl.pallas_call(
        functools.partial(up_kernel, len(pieces), half),
        in_specs=[SMEM] + [ANY] * len(pieces) + [HBM] * (len(nears) + len(fars)),
        out_specs=VMEM,
        out_shape=jax.ShapeDtypeStruct((rows, width), BF),
        scratch_shapes=[
            pltpu.VMEM((rows, depth), BF),
            pltpu.VMEM((NZ, count, rows_in, width), BF),
            pltpu.SemaphoreType.DMA((len(pieces),)),
            pltpu.SemaphoreType.DMA((NZ, len(fars))),
        ],
        compiler_params=params(SMALL_LIMIT),
    )(pos, *pieces, *nears, *fars)


def join_copies(places, pos, parts, out, sem):
    z, y, m = pos[0], pos[1], pos[2]
    share = out.shape[0] // NM
    copies = []
    for part, (side, half, devices) in zip(parts, places):
        width = part.shape[1]
        columns = pl.ds(pl.multiple_of(((y ^ side) * 2 + (z % 2 ^ half)) * width, width), width)
        for i, r in enumerate(devices):
            rows = pl.ds(pl.multiple_of((m ^ r) * share, 16), share)
            src = part.at[i * share : (i + 1) * share]
            copies.append(pltpu.make_async_copy(src, out.at[rows, columns], sem.at[len(copies)]))
    return copies


def join_kernel(places, pos, *refs):
    *parts, out, sem = refs
    copies = join_copies(places, pos, parts[-len(places) :], out, sem)
    for copy in copies:
        copy.start()
    for copy in copies:
        copy.wait()


def join_parts(pos, shape, parts, before=None):
    places = [part[1:] for part in parts]
    started = [] if before is None else [before]
    return pl.pallas_call(
        functools.partial(join_kernel, places),
        in_specs=[SMEM] + [HBM] * len(started) + [ANY] * len(parts),
        out_specs=HBM,
        out_shape=jax.ShapeDtypeStruct(shape, BF),
        scratch_shapes=[pltpu.SemaphoreType.DMA((sum(len(devices) for _, _, devices in places),))],
        input_output_aliases={1: 0} if started else {},
        compiler_params=params(SMALL_LIMIT),
    )(pos, *started, *(part[0] for part in parts))


def pages_kernel(pos, table, own, got, out):
    y = pos[1]
    for b in range(own.shape[0]):
        slot = table[0, b]
        for side, part in ((0, own), (1, got)):
            for h in range(HEADS):
                out[slot, :, (y ^ side) * HEADS + h] = part[b, :, h]


def place_pages(pos, table, own, got):
    blocks, two, heads, page, width = own.shape
    return pl.pallas_call(
        pages_kernel,
        in_specs=[SMEM, SMEM, VMEM, VMEM],
        out_specs=VMEM,
        out_shape=jax.ShapeDtypeStruct((blocks, two, NY * heads, page, width), BF),
        compiler_params=params(SMALL_LIMIT),
    )(pos, table, own, got)


def in_quad(copies):
    return lax.all_to_all(copies, AXES, split_axis=0, concat_axis=0, tiled=True, axis_index_groups=QUADS)


def local_planes(hidden_in, segment_ids, page_table, qkv_master, up_master, dense_weight):
    dp, mp = lax.axis_index("dp"), lax.axis_index("mp")
    z, y = dp // NY, dp % NY
    pos = jnp.stack([z, y, mp]).astype(jnp.int32)
    share = hidden_in.shape[0]
    head = H // NM * mp + HEADS * y + jnp.arange(HEADS)
    slopes = jnp.exp2(-8.0 * (head + 1).astype(F32) / H)

    qkv_own = to_all(cast_pieces(qkv_master))
    up_0, up_1, normed = cast_and_norm(pos, up_master, hidden_in)
    raw_0 = send(up_1, ZSWAP)
    from_y = send(normed, YSWAP)
    from_x = send(normed, XSWAP)
    cross_low = send(from_y[: share // 2], XSWAP)
    cross_high = send(from_x[share // 2 :], YSWAP)
    tokens = [normed, from_y, from_x, cross_low, cross_high]
    half = dense_weight.shape[0] // 2
    give = lax.dynamic_slice_in_dim(dense_weight, y * half, half, 0)
    give_far = lax.dynamic_slice_in_dim(dense_weight, (1 - y) * half + half // 2, half // 2, 0)
    seg_other = send(segment_ids, YSWAP)
    segments = jnp.concatenate([segment_ids, seg_other], 0)
    seg_rows = segments[:, None, :]
    qkv_own, up_0, up_1, raw_0, give, give_far, seg_rows, slopes, pos, dense_own, *tokens = window(
        qkv_own, up_0, up_1, raw_0, give, give_far, seg_rows, slopes, pos, dense_weight, *tokens
    )

    qkv_got = send(qkv_own, ZSWAP)
    near_0 = in_plane(stack_rows(up_0, raw_0))
    near = send(give, XSWAP)
    dense_c = send(dense_own, CORE)
    tokens += [send(piece, CORE) for piece in tokens]
    before = one_head(pos, slopes, seg_rows, tokens, qkv_own)
    qkv_got, near_0, up_1, near, give_far, dense_own, dense_c, *state = window(
        qkv_got, near_0, up_1, near, give_far, dense_own, dense_c, *tokens, *before
    )
    tokens, before = state[:TOKEN_PIECES], state[TOKEN_PIECES:]

    part = PLANE // 2
    far_a = send(near_0[:part], ZFAR)
    near_got = send(near_0[:, : near_0.shape[1] // 2], ZSWAP)
    far_y = send(near[: half // 2], YSWAP)
    far_x = send(give_far, XSWAP)
    context, kv_own, kv_other = one_head(pos, slopes, seg_rows, tokens, qkv_got, before)
    ctx_own = in_plane(context.reshape(PLANE, -1, HEADS * HD))
    kv_got = send(kv_other, YSWAP)
    near_0, near_got, up_1, far_a, ctx_own, near, far_y, far_x, dense_own, dense_c, kv_own, kv_got = window(
        near_0, near_got, up_1, far_a, ctx_own, near, far_y, far_x, dense_own, dense_c, kv_own, kv_got
    )

    far_b = send(near_0[part:], ZFAR)
    near_own = in_plane(up_1)
    got_a = send(far_a, ZSWAP)
    blocks = [dense_own, dense_c, near, far_y, far_x]
    blocks += [send(block, CORE) for block in blocks[2:]]
    hidden_out, normed = dense_norm(pos, hidden_in, ctx_own, blocks)
    from_y = send(normed, YSWAP)
    from_x = send(normed, XSWAP)
    near_0, near_own, near_got, far_a, far_b, got_a, normed, from_y, from_x, kv_own, kv_got = window(
        near_0, near_own, near_got, far_a, far_b, got_a, normed, from_y, from_x, kv_own, kv_got
    )

    got_b = send(far_b, ZSWAP)
    cross_low = send(from_y[: share // 2], XSWAP)
    cross_high = send(from_x[share // 2 :], YSWAP)
    other = [from_y, cross_low, cross_high]
    other += [send(piece, CORE) for piece in other]
    own = [normed, from_x, send(normed, CORE), send(from_x, CORE)]
    *tokens, near_0, far_a, far_b = window(*other, *own, near_0, far_a, far_b)
    other, own = tokens[:6], tokens[6:]
    weights = [((near_0,), (far_a, far_b)), ((near_own, near_got), (got_a, got_b))]
    parts = []
    done = pos
    for half, side, pieces in ((0, 1, other), (1, 1, other), (0, 0, own), (1, 0, own)):
        first, _ = window(pieces[0], done)
        done = up_part(pos, half, [first] + pieces[1:], *weights[half])
        parts.append((send(done, YSWAP) if side else done, side, half, (0, 2, 1, 3)))
    shape = (NM * share, up_master.shape[1] // NM)
    activated = join_parts(pos, shape, [parts[0]] + parts[2:])
    activated = join_parts(pos, shape, parts[1:2], activated)
    cache = place_pages(pos, page_table, kv_own, kv_got)
    return hidden_out, activated, cache


def solution(mesh):
    placed = (
        P(("dp", "mp"), None),
        P("dp", None),
        P("dp", None),
        P(("dp", "mp"), None),
        P(("dp", "mp"), None),
        P("mp", None),
    )
    planes = mesh.shape["dp"] == NZ * NY and mesh.shape["mp"] == NM
    return jax.shard_map(
        local_planes if planes else local_any,
        mesh=mesh,
        in_specs=placed,
        out_specs=(P(("dp", "mp"), None), P("dp", "mp"), P("dp", None, "mp", None, None)),
        check_vma=False,
    )
```

```python
import functools

import jax
import jax.numpy as jnp
from jax import lax
from jax.experimental import pallas as pl
from jax.experimental.pallas import tpu as pltpu
from jax.sharding import PartitionSpec as P

H = 16
HD = 128
PAGE = 128
AXES = ("dp", "mp")
BF = jnp.bfloat16
F32 = jnp.float32
VMEM_LIMIT = 50 * 1024 * 1024
SMALL_LIMIT = 12 * 1024 * 1024


def layer_norm(values):
    mean_val = jnp.mean(values, -1, keepdims=True)
    centered = values - mean_val
    variance = jnp.mean(centered * centered, -1, keepdims=True)
    return centered * lax.rsqrt(variance + 1e-05)


def attend(normed, qkv_w, segment, table, mp_index):
    group_rows = normed.shape[0]
    heads_dev = qkv_w.shape[1] // (3 * HD)
    joined = jnp.dot(normed, qkv_w, preferred_element_type=F32).astype(BF)
    joined = joined.reshape(group_rows, heads_dev, 3, HD)
    query = joined[:, :, 0]
    keys = joined[:, :, 1]
    vals = joined[:, :, 2]
    head_ids = mp_index * heads_dev + jnp.arange(heads_dev)
    slopes = jnp.exp2(-8.0 * (head_ids + 1).astype(F32) / H)
    positions = jnp.arange(group_rows)
    distance = (positions[:, None] - positions[None, :]).astype(F32)
    allowed = (segment[:, None] == segment[None, :]) & (distance >= 0)
    scores = jnp.einsum("thd,shd->hts", query, keys, preferred_element_type=F32) / jnp.sqrt(F32(HD))
    scores = scores - slopes[:, None, None] * distance[None]
    scores = jnp.where(allowed[None], scores, -jnp.inf)
    probs = jax.nn.softmax(scores, axis=-1).astype(BF)
    context = jnp.einsum("hts,shd->thd", probs, vals, preferred_element_type=F32).astype(BF)
    context = context.reshape(group_rows, heads_dev * HD)
    key_vals = jnp.stack([keys, vals], 1)
    pages_here = group_rows // PAGE
    key_vals = key_vals.reshape(pages_here, PAGE, 2, heads_dev, HD).transpose(0, 2, 3, 1, 4)
    cache = jnp.zeros((pages_here, 2, heads_dev, PAGE, HD), BF).at[table].set(key_vals)
    return context, cache


def local_any(hidden_in, segment_ids, page_table, qkv_master, up_master, dense_weight):
    mp_index = lax.axis_index("mp")

    def columns(master):
        mine = lax.all_to_all(master.astype(BF), "mp", split_axis=1, concat_axis=0, tiled=True)
        return lax.all_gather(mine, "dp", axis=0, tiled=True)

    qkv_w = columns(qkv_master)
    up_w = columns(up_master)
    normed_own = layer_norm(hidden_in.astype(F32)).astype(BF)
    normed = lax.all_gather(normed_own, "mp", axis=0, tiled=True)
    context, cache = attend(normed, qkv_w, segment_ids[0], page_table[0], mp_index)
    term = jnp.dot(context, dense_weight, preferred_element_type=F32).astype(BF)
    share = lax.psum_scatter(term, "mp", scatter_dimension=0, tiled=True).astype(F32)
    stream_own = hidden_in.astype(F32) + share
    normed_two = lax.all_gather(layer_norm(stream_own).astype(BF), "mp", axis=0, tiled=True)
    upper = jnp.dot(normed_two, up_w, preferred_element_type=F32)
    activated = jax.nn.gelu(upper, approximate=True).astype(BF)
    return stream_own.astype(BF), activated, cache


NZ, NY, NM = 4, 2, 4
PLANE = NY * NM
HEADS = H // PLANE


def pairs(move):
    out = []
    for z in range(NZ):
        for y in range(NY):
            for m in range(NM):
                to = move(z, y, m)
                if to is not None:
                    out.append(((z * NY + y) * NM + m, (to[0] * NY + to[1]) * NM + to[2]))
    return out


CORE = pairs(lambda z, y, m: (z, y, m ^ 1))
XSWAP = pairs(lambda z, y, m: (z, y, m ^ 2))
YSWAP = pairs(lambda z, y, m: (z, y ^ 1, m))
ZSWAP = pairs(lambda z, y, m: (z ^ 1, y, m))
ZFAR = pairs(lambda z, y, m: (z ^ 2, y, m))
PLANES = [[z * PLANE + i for i in range(PLANE)] for z in range(NZ)]
QUADS = [[z * PLANE + 2 * i + c for i in range(PLANE // 2)] for z in range(NZ) for c in range(2)]


def send(value, moves):
    return lax.ppermute(value, AXES, moves)


def window(*values):
    return lax.optimization_barrier(values)


def params(limit=VMEM_LIMIT):
    return pltpu.CompilerParams(vmem_limit_bytes=limit)


HBM = pl.BlockSpec(memory_space=pltpu.HBM)
ANY = pl.BlockSpec(memory_space=pl.ANY)
SMEM = pl.BlockSpec(memory_space=pltpu.SMEM)
VMEM = pl.BlockSpec(memory_space=pltpu.VMEM)


def cast_pieces(master):
    rows, cols = master.shape
    width = cols // PLANE // 2

    def kernel(src, dst):
        for p in range(PLANE):
            for part in range(2):
                start = ((2 * (p % NM) + p // NM) * 2 + part) * width
                piece = src[:, start : start + width].astype(BF)
                for z in range(part, NZ, 2):
                    dst[z * PLANE + p] = piece

    return pl.pallas_call(
        kernel,
        in_specs=[VMEM],
        out_specs=VMEM,
        out_shape=jax.ShapeDtypeStruct((NZ * PLANE, rows, width), BF),
        compiler_params=params(),
    )(master)


def cast_and_norm(pos, master, hidden):
    rows, cols = master.shape
    half = cols // PLANE // 2

    def kernel(pos, src, hidden, first, second, normed):
        parity = pos[0] % 2
        for p in range(PLANE):
            start = (2 * (p % NM) + p // NM) * 2 * half
            for i, dst in ((0, first), (1, second)):
                column = pl.multiple_of(start + (parity ^ i) * half, half)
                dst[p] = src[:, pl.ds(column, half)].astype(BF)
        normed[...] = layer_norm(hidden[...].astype(F32)).astype(BF)

    shape = jax.ShapeDtypeStruct((PLANE, rows, half), BF)
    return pl.pallas_call(
        kernel,
        in_specs=[SMEM, VMEM, VMEM],
        out_specs=[VMEM, VMEM, VMEM],
        out_shape=[shape, shape, jax.ShapeDtypeStruct(hidden.shape, BF)],
        compiler_params=params(),
    )(pos, master, hidden)


def stack_kernel(own, got, out):
    rows = own.shape[1]
    out[:, :rows] = own[...]
    out[:, rows:] = got[...]


def stack_rows(own, got):
    count, rows, width = own.shape
    return pl.pallas_call(
        stack_kernel,
        in_specs=[VMEM, VMEM],
        out_specs=VMEM,
        out_shape=jax.ShapeDtypeStruct((count, 2 * rows, width), BF),
        compiler_params=params(),
    )(own, got)


def to_all(pieces):
    mine = lax.all_to_all(pieces, AXES, split_axis=0, concat_axis=0, tiled=True)
    return mine.reshape(-1, mine.shape[2])


def in_plane(pieces):
    return lax.all_to_all(pieces, AXES, split_axis=0, concat_axis=0, tiled=True, axis_index_groups=PLANES)


TOKEN_PIECES = 10


def token_copies(y, m, pieces, xbuf, sem):
    share = pieces[0].shape[0]
    half = share // 2
    place = [(0, 0, 0), (1, 0, 0), (0, 2, 0), (1, 2, 0), (1, 2, half)]
    place += [(dy, dm ^ 1, extra) for dy, dm, extra in place]
    copies = []
    for i, (dy, dm, extra) in enumerate(place):
        first = pl.multiple_of(((y ^ dy) * NM + (m ^ dm)) * share + extra, 16)
        copies.append(pltpu.make_async_copy(pieces[i], xbuf.at[pl.ds(first, pieces[i].shape[0])], sem.at[i]))
    return copies


def head_kernel(last, pos, slope, seg_rows, *refs):
    pieces, refs = refs[:TOKEN_PIECES], refs[TOKEN_PIECES:]
    if last:
        before, refs = refs[:3], refs[3:]
    weights, ctx, kv_own, kv_other, xbuf, wbuf, xsem, wsem = refs
    z, y, m = pos[0], pos[1], pos[2]
    copies = [pltpu.make_async_copy(weights, wbuf, wsem)] + token_copies(y, m, pieces, xbuf, xsem)
    for copy in copies:
        copy.start()
    group = xbuf.shape[0] // NY
    here = lax.broadcasted_iota(jnp.int32, (group, group), 0)
    there = lax.broadcasted_iota(jnp.int32, (group, group), 1)
    distance = here - there
    away = distance.astype(F32)
    h = 1 - z % 2 if last else z % 2
    if last:
        for src, dst in zip(before, (ctx, kv_own, kv_other)):
            dst[...] = src[...]
    for copy in copies:
        copy.wait()
    for g, kv in ((0, kv_own), (1, kv_other)):
        rows = pl.ds(pl.multiple_of((y ^ g) * group, group), group)
        seg_cols = jnp.broadcast_to(seg_rows[g], (PAGE, group)).T[:, :1]
        allowed = (seg_cols == seg_rows[g]) & (distance >= 0)
        joined = jnp.dot(xbuf[rows, :], wbuf[...], preferred_element_type=F32).astype(BF)
        query, keys, vals = (joined[:, j * HD : (j + 1) * HD] for j in range(3))
        scores = lax.dot_general(query, keys, (((1,), (1,)), ((), ())), preferred_element_type=F32)
        scores = scores * (1.0 / HD**0.5) - slope[h] * away
        scores = jnp.where(allowed, scores, -jnp.inf)
        raised = jnp.exp(scores - jnp.max(scores, -1, keepdims=True))
        probs = (raised * (1.0 / jnp.sum(raised, -1, keepdims=True))).astype(BF)
        result = jnp.dot(probs, vals, preferred_element_type=F32).astype(BF)
        ctx[rows, pl.ds(pl.multiple_of(h * HD, HD), HD)] = result
        for b in range(group // PAGE):
            kv[b, 0, h] = keys[b * PAGE : (b + 1) * PAGE]
            kv[b, 1, h] = vals[b * PAGE : (b + 1) * PAGE]


def one_head(pos, slope, seg_rows, tokens, weights, before=()):
    count, depth = PLANE * tokens[0].shape[0], tokens[0].shape[1]
    width = weights.shape[1]
    kv_shape = jax.ShapeDtypeStruct((count // NY // PAGE, 2, HEADS, PAGE, HD), BF)
    return pl.pallas_call(
        functools.partial(head_kernel, bool(before)),
        in_specs=[SMEM, SMEM, VMEM] + [ANY] * TOKEN_PIECES + [VMEM] * len(before) + [HBM],
        out_specs=[VMEM, VMEM, VMEM],
        out_shape=[jax.ShapeDtypeStruct((count, HEADS * HD), BF), kv_shape, kv_shape],
        scratch_shapes=[
            pltpu.VMEM((count, depth), BF),
            pltpu.VMEM((depth, width), BF),
            pltpu.SemaphoreType.DMA((TOKEN_PIECES,)),
            pltpu.SemaphoreType.DMA,
        ],
        compiler_params=params(),
    )(pos, slope, seg_rows, *tokens, *before, weights)


def dense_kernel(pos, hidden, ctx, own, cross, *rest):
    rows, (out, normed, dense, sem) = rest[:6], rest[6:]
    y, m = pos[1], pos[2]
    size = own.shape[0]
    half = size // 2
    loads = [[pltpu.make_async_copy(own, dense.at[0], sem.at[0])], [pltpu.make_async_copy(cross, dense.at[1], sem.at[1])]]
    for r in (2, 3):
        copies = []
        for i, first in enumerate((y * half, (1 - y) * half, (1 - y) * half + half // 2)):
            index = (r - 2) * 3 + i
            dst = dense.at[r, pl.ds(pl.multiple_of(first, half // 2), rows[index].shape[0])]
            copies.append(pltpu.make_async_copy(rows[index], dst, sem.at[2 + index]))
        loads.append(copies)
    for copies in loads:
        for copy in copies:
            copy.start()
    total = None
    for r in range(NM):
        owner = m ^ r
        left = jnp.concatenate([ctx[owner], ctx[NM + owner]], axis=1)
        for copy in loads[r]:
            copy.wait()
        term = jnp.dot(left, dense[r], preferred_element_type=F32).astype(BF).astype(F32)
        total = term if total is None else total + term
    stream = hidden[...].astype(F32) + total
    out[...] = stream.astype(BF)
    normed[...] = layer_norm(stream).astype(BF)


def dense_norm(pos, hidden, ctx, blocks):
    return pl.pallas_call(
        dense_kernel,
        in_specs=[SMEM, VMEM, VMEM] + [HBM] * 2 + [ANY] * (len(blocks) - 2),
        out_specs=[VMEM, VMEM],
        out_shape=[jax.ShapeDtypeStruct(hidden.shape, BF)] * 2,
        scratch_shapes=[
            pltpu.VMEM((NM,) + blocks[0].shape, BF),
            pltpu.SemaphoreType.DMA((len(blocks),)),
        ],
        compiler_params=params(),
    )(pos, hidden, ctx, *blocks)


def up_kernel(count, half, pos, *refs):
    pieces, (*nears, far_a, far_b), (act, xbuf, wbuf, xsem, wsem) = refs[:count], refs[count:-5], refs[-5:]
    z = pos[0]
    fars = (far_a, far_b)
    rows, width = wbuf.shape[2], wbuf.shape[3]
    loads = [[] for _ in range(NZ)]
    for side in range(2):
        src = nears[side] if len(nears) == 2 else nears[0].at[:, side * rows : (side + 1) * rows]
        loads[side].append(pltpu.make_async_copy(src, wbuf.at[side], wsem.at[side, 0]))
        r = 2 + (side ^ half)
        at = 0
        for i, far in enumerate(fars):
            dst = wbuf.at[r, at : at + far.shape[0]]
            loads[r].append(pltpu.make_async_copy(far.at[:, side * rows : (side + 1) * rows], dst, wsem.at[r, i]))
            at += far.shape[0]
    copies = []
    at = 0
    for i, piece in enumerate(pieces):
        copies.append(pltpu.make_async_copy(piece, xbuf.at[at : at + piece.shape[0]], xsem.at[i]))
        at += piece.shape[0]
    for copy in copies + [load for group in loads for load in group]:
        copy.start()
    for copy in copies:
        copy.wait()
    depth = wbuf.shape[1] * rows
    upper = None
    for r in range(NZ):
        for load in loads[r]:
            load.wait()
        left = xbuf[:, pl.ds(pl.multiple_of((z ^ r) * depth, depth), depth)]
        term = jnp.dot(left, wbuf[r].reshape(depth, width), preferred_element_type=F32)
        upper = term if upper is None else upper + term
    act[...] = jax.nn.gelu(upper, approximate=True).astype(BF)


def up_part(pos, half, pieces, nears, fars):
    rows, depth = sum(piece.shape[0] for piece in pieces), pieces[0].shape[1]
    count, rows_in, width = 2 * fars[0].shape[0], fars[0].shape[1] // 2, nears[0].shape[2]
    return pl.pallas_call(
        functools.partial(up_kernel, len(pieces), half),
        in_specs=[SMEM] + [ANY] * len(pieces) + [HBM] * (len(nears) + len(fars)),
        out_specs=VMEM,
        out_shape=jax.ShapeDtypeStruct((rows, width), BF),
        scratch_shapes=[
            pltpu.VMEM((rows, depth), BF),
            pltpu.VMEM((NZ, count, rows_in, width), BF),
            pltpu.SemaphoreType.DMA((len(pieces),)),
            pltpu.SemaphoreType.DMA((NZ, len(fars))),
        ],
        compiler_params=params(SMALL_LIMIT),
    )(pos, *pieces, *nears, *fars)


def join_copies(places, pos, parts, out, sem):
    z, y, m = pos[0], pos[1], pos[2]
    share = out.shape[0] // NM
    copies = []
    for part, (side, half, devices) in zip(parts, places):
        width = part.shape[1]
        columns = pl.ds(pl.multiple_of(((y ^ side) * 2 + (z % 2 ^ half)) * width, width), width)
        for i, r in enumerate(devices):
            rows = pl.ds(pl.multiple_of((m ^ r) * share, 16), share)
            src = part.at[i * share : (i + 1) * share]
            copies.append(pltpu.make_async_copy(src, out.at[rows, columns], sem.at[len(copies)]))
    return copies


def join_kernel(places, pos, *refs):
    *parts, out, sem = refs
    copies = join_copies(places, pos, parts[-len(places) :], out, sem)
    for copy in copies:
        copy.start()
    for copy in copies:
        copy.wait()


def join_parts(pos, shape, parts, before=None):
    places = [part[1:] for part in parts]
    started = [] if before is None else [before]
    return pl.pallas_call(
        functools.partial(join_kernel, places),
        in_specs=[SMEM] + [HBM] * len(started) + [ANY] * len(parts),
        out_specs=HBM,
        out_shape=jax.ShapeDtypeStruct(shape, BF),
        scratch_shapes=[pltpu.SemaphoreType.DMA((sum(len(devices) for _, _, devices in places),))],
        input_output_aliases={1: 0} if started else {},
        compiler_params=params(SMALL_LIMIT),
    )(pos, *started, *(part[0] for part in parts))


def pages_kernel(pos, table, own, got, out):
    y = pos[1]
    for b in range(own.shape[0]):
        slot = table[0, b]
        for side, part in ((0, own), (1, got)):
            for h in range(HEADS):
                out[slot, :, (y ^ side) * HEADS + h] = part[b, :, h]


def place_pages(pos, table, own, got):
    blocks, two, heads, page, width = own.shape
    return pl.pallas_call(
        pages_kernel,
        in_specs=[SMEM, SMEM, VMEM, VMEM],
        out_specs=VMEM,
        out_shape=jax.ShapeDtypeStruct((blocks, two, NY * heads, page, width), BF),
        compiler_params=params(SMALL_LIMIT),
    )(pos, table, own, got)


def in_quad(copies):
    return lax.all_to_all(copies, AXES, split_axis=0, concat_axis=0, tiled=True, axis_index_groups=QUADS)


def local_planes(hidden_in, segment_ids, page_table, qkv_master, up_master, dense_weight):
    dp, mp = lax.axis_index("dp"), lax.axis_index("mp")
    z, y = dp // NY, dp % NY
    pos = jnp.stack([z, y, mp]).astype(jnp.int32)
    share = hidden_in.shape[0]
    head = H // NM * mp + HEADS * y + jnp.arange(HEADS)
    slopes = jnp.exp2(-8.0 * (head + 1).astype(F32) / H)

    qkv_own = to_all(cast_pieces(qkv_master))
    up_0, up_1, normed = cast_and_norm(pos, up_master, hidden_in)
    raw_0 = send(up_1, ZSWAP)
    from_y = send(normed, YSWAP)
    from_x = send(normed, XSWAP)
    cross_low = send(from_y[: share // 2], XSWAP)
    cross_high = send(from_x[share // 2 :], YSWAP)
    tokens = [normed, from_y, from_x, cross_low, cross_high]
    half = dense_weight.shape[0] // 2
    give = lax.dynamic_slice_in_dim(dense_weight, y * half, half, 0)
    give_far = lax.dynamic_slice_in_dim(dense_weight, (1 - y) * half + half // 2, half // 2, 0)
    seg_other = send(segment_ids, YSWAP)
    segments = jnp.concatenate([segment_ids, seg_other], 0)
    seg_rows = segments[:, None, :]
    qkv_own, up_0, up_1, raw_0, give, give_far, seg_rows, slopes, pos, dense_own, *tokens = window(
        qkv_own, up_0, up_1, raw_0, give, give_far, seg_rows, slopes, pos, dense_weight, *tokens
    )

    qkv_got = send(qkv_own, ZSWAP)
    near_0 = in_plane(stack_rows(up_0, raw_0))
    near = send(give, XSWAP)
    dense_c = send(dense_own, CORE)
    tokens += [send(piece, CORE) for piece in tokens]
    before = one_head(pos, slopes, seg_rows, tokens, qkv_own)
    qkv_got, near_0, up_1, near, give_far, dense_own, dense_c, *state = window(
        qkv_got, near_0, up_1, near, give_far, dense_own, dense_c, *tokens, *before
    )
    tokens, before = state[:TOKEN_PIECES], state[TOKEN_PIECES:]

    part = PLANE // 2
    far_a = send(near_0[:part], ZFAR)
    near_got = send(near_0[:, : near_0.shape[1] // 2], ZSWAP)
    far_y = send(near[: half // 2], YSWAP)
    far_x = send(give_far, XSWAP)
    context, kv_own, kv_other = one_head(pos, slopes, seg_rows, tokens, qkv_got, before)
    ctx_own = in_plane(context.reshape(PLANE, -1, HEADS * HD))
    kv_got = send(kv_other, YSWAP)
    near_0, near_got, up_1, far_a, ctx_own, near, far_y, far_x, dense_own, dense_c, kv_own, kv_got = window(
        near_0, near_got, up_1, far_a, ctx_own, near, far_y, far_x, dense_own, dense_c, kv_own, kv_got
    )

    far_b = send(near_0[part:], ZFAR)
    near_own = in_plane(up_1)
    got_a = send(far_a, ZSWAP)
    blocks = [dense_own, dense_c, near, far_y, far_x]
    blocks += [send(block, CORE) for block in blocks[2:]]
    hidden_out, normed = dense_norm(pos, hidden_in, ctx_own, blocks)
    from_y = send(normed, YSWAP)
    from_x = send(normed, XSWAP)
    near_0, near_own, near_got, far_a, far_b, got_a, normed, from_y, from_x, kv_own, kv_got = window(
        near_0, near_own, near_got, far_a, far_b, got_a, normed, from_y, from_x, kv_own, kv_got
    )

    got_b = send(far_b, ZSWAP)
    cross_low = send(from_y[: share // 2], XSWAP)
    cross_high = send(from_x[share // 2 :], YSWAP)
    other = [from_y, cross_low, cross_high]
    other += [send(piece, CORE) for piece in other]
    own = [normed, from_x, send(normed, CORE), send(from_x, CORE)]
    *tokens, near_0, far_a, far_b = window(*other, *own, near_0, far_a, far_b)
    other, own = tokens[:6], tokens[6:]
    weights = [((near_0,), (far_a, far_b)), ((near_own, near_got), (got_a, got_b))]
    parts = []
    done = pos
    for half, side, pieces in ((0, 1, other), (1, 1, other), (0, 0, own), (1, 0, own)):
        first, _ = window(pieces[0], done)
        done = up_part(pos, half, [first] + pieces[1:], *weights[half])
        parts.append((send(done, YSWAP) if side else done, side, half, (0, 2, 1, 3)))
    shape = (NM * share, up_master.shape[1] // NM)
    activated = join_parts(pos, shape, [parts[0]] + parts[2:])
    activated = join_parts(pos, shape, parts[1:2], activated)
    cache = place_pages(pos, page_table, kv_own, kv_got)
    return hidden_out, activated, cache


def solution(mesh):
    placed = (
        P(("dp", "mp"), None),
        P("dp", None),
        P("dp", None),
        P(("dp", "mp"), None),
        P(("dp", "mp"), None),
        P("mp", None),
    )
    planes = mesh.shape["dp"] == NZ * NY and mesh.shape["mp"] == NM
    return jax.shard_map(
        local_planes if planes else local_any,
        mesh=mesh,
        in_specs=placed,
        out_specs=(P(("dp", "mp"), None), P("dp", "mp"), P("dp", None, "mp", None, None)),
        check_vma=False,
    )
```
